128 devices in a mesh: seq: 32 (over y, z, x_hi), head: 4 (over x_lo, core).
Axes of the slice: x: 4 (x_hi: 2, x_lo: 2; x = x_hi * 2 + x_lo), y: 4, z: 4, core: 2. Of those that a mesh axis runs over, the one named last changes fastest.
Arguments:
- query: bfloat16 [12288, 1024], P('seq', 'head'), may hold values from -6 to 6
- key: bfloat16 [12288, 1024], P('seq', 'head'), may hold values from -6 to 6
- value: bfloat16 [12288, 1024], P('seq', 'head'), may hold values from -6 to 6
- attn_out: bfloat16 [12288, 1024], P('seq', 'head'), may hold values from -4 to 4
- log_norm: float32 [16, 12288], P('head', 'seq')
- d_output: bfloat16 [12288, 1024], P('seq', 'head'), may hold values from -2 to 2
- out_weight: bfloat16 [1024, 1024], P('head'), may hold values from -0.1875 to 0.1875
- coords: bfloat16 [3, 12288], P(None, 'seq'), may hold values from -5 to 5
- slopes: float32 [16], P('head'), may hold values from 0.05 to 2, as said below
Outputs:
- d_query: bfloat16 [12288, 1024], P('seq', 'head')
- d_key: bfloat16 [12288, 1024], P('seq', 'head')
- d_value: bfloat16 [12288, 1024], P('seq', 'head')
- d_out_weight: float32 [1024, 1024], P('head')
- d_slopes: float32 [16], P('head')
The draws below stay inside these ranges and needn't reach their ends.
Inputs may be any that keep to these rules, and one draw needn't show every extreme that they name: slopes: one rate a head.
All inputs are finite; a program needn't handle non-finite values.
Results may differ from the reference program's by a relative error of at most 0.023.
Values may be sent and summed in bfloat16 or wider, within the bound.
A program may use at most 64 MiB of HBM per device.

```python
import math
import jax
import jax.numpy as jnp
from jax import lax

D = 1024
HEADS = 16
HEAD_DIM = 64
ROWS = 384
NODES = 12288


def rate_values(base_key):
    sub_key = jax.random.fold_in(base_key, 11)
    return jnp.exp(jax.random.uniform(sub_key, (HEADS,), jnp.float32, math.log(0.05), math.log(2.0)))


def draw_slopes(key, part):
    rates = rate_values(key)
    return rates


def draw_log_norm(key, part):
    rates = rate_values(key)
    key = jax.random.fold_in(key, 2)
    jitter = jax.random.uniform(key, (HEADS, NODES), jnp.float32, -0.5, 0.5)
    return math.log(NODES) + 0.5 - 2.5 * rates[:, None] + jitter


def block_scale(own_key, shape, pieces, smallest, top_value):
    loudness, own = 1.0, jax.random.fold_in(own_key, 6)
    for dim, blocks in pieces:
        steps = jnp.exp(jax.random.uniform(jax.random.fold_in(own, dim), (blocks,), jnp.float32, smallest / len(pieces), top_value / len(pieces)))
        loudness = loudness * jnp.repeat(steps, shape[dim] // blocks).reshape([-1 if axis == dim else 1 for axis in range(len(shape))])
    return loudness


def bell_draw(own_key, extent, spread, reach, shards=(), kind=jnp.bfloat16):
    drawn = spread * jax.random.normal(own_key, extent, jnp.float32)
    if shards:
        drawn = drawn * block_scale(own_key, extent, shards, -0.22, 0.18)
    return jnp.clip(drawn, -reach, reach).astype(kind)


def setup_inputs(seed: int = 0) -> dict:
    key_of = jax.random.split(jax.random.key(seed), 10)
    return {
        "query": bell_draw(key_of[0], (NODES, HEADS * HEAD_DIM), 1.0, 6.0, ((0, 32), (1, 4))),
        "key": bell_draw(key_of[1], (NODES, HEADS * HEAD_DIM), 1.0, 6.0, ((0, 32), (1, 4))),
        "value": bell_draw(key_of[2], (NODES, HEADS * HEAD_DIM), 1.0, 6.0, ((0, 32), (1, 4))),
        "attn_out": bell_draw(key_of[3], (NODES, HEADS * HEAD_DIM), 0.5, 4.0, ((0, 32), (1, 4))),
        "log_norm": draw_log_norm(jax.random.fold_in(key_of[9], 71), 0),
        "d_output": bell_draw(key_of[5], (NODES, D), 0.25, 2.0, ((0, 32), (1, 4))),
        "out_weight": bell_draw(key_of[6], (HEADS * HEAD_DIM, D), (HEADS * HEAD_DIM) ** -0.5, 0.1875, ((0, 4),)),
        "coords": bell_draw(key_of[7], (3, NODES), 1.0, 5.0, ((1, 32),)),
        "slopes": draw_slopes(jax.random.fold_in(key_of[9], 71), 0),
    }


def distance(mine, theirs):
    total = jnp.ones((mine.shape[1], theirs.shape[1]), jnp.float32)
    for component in range(3):
        offset = mine[component].astype(jnp.float32)[:, None] - theirs[component].astype(jnp.float32)[None, :]
        total = total + offset * offset
    return jnp.sqrt(total)

def reference(query, key, value, attn_out, log_norm, d_output, out_weight, coords, slopes):
    nodes = query.shape[0]
    scale = HEAD_DIM ** (-0.5)
    d_attn = jnp.dot(d_output, out_weight.T, preferred_element_type=jnp.float32).astype(jnp.bfloat16)
    d_out_weight = jnp.dot(attn_out.T, d_output, preferred_element_type=jnp.float32)

    def by_heads(array):
        return array.reshape(nodes, HEADS, HEAD_DIM).transpose(1, 0, 2)
    row_delta = lax.optimization_barrier(jnp.sum(by_heads(d_attn).astype(jnp.float32) * by_heads(attn_out).astype(jnp.float32), axis=2))
    blocks = nodes // ROWS

    def one_head(items):
        query_h, key_h, value_h, dout_h, delta_h, norm_h, head_rate = items

        def visit(carry, index):
            query_grad, slope_grad = carry
            start = (index * ROWS).astype(jnp.int32)
            key_blk = lax.dynamic_slice_in_dim(key_h, start, ROWS, 0)
            val_blk = lax.dynamic_slice_in_dim(value_h, start, ROWS, 0)
            pos_blk = lax.dynamic_slice_in_dim(coords, start, ROWS, 1)
            lengths = distance(coords, pos_blk)
            scores = jnp.dot(query_h, key_blk.T, preferred_element_type=jnp.float32)
            attn_probs = jnp.exp(scores * scale - head_rate * lengths - norm_h[:, None])
            probs_b = attn_probs.astype(jnp.bfloat16)
            value_grad = jnp.dot(probs_b.T, dout_h, preferred_element_type=jnp.float32)
            grad_probs = jnp.dot(dout_h, val_blk.T, preferred_element_type=jnp.float32)
            grad_scores = attn_probs * (grad_probs - delta_h[:, None])
            slope_grad = slope_grad - jnp.sum(grad_scores * lengths)
            grad_b = grad_scores.astype(jnp.bfloat16)
            query_grad = query_grad + jnp.dot(grad_b, key_blk, preferred_element_type=jnp.float32) * scale
            key_grad = jnp.dot(grad_b.T, query_h, preferred_element_type=jnp.float32) * scale
            return ((query_grad, slope_grad), (key_grad, value_grad))
        initial = (jnp.zeros((nodes, HEAD_DIM), jnp.float32), jnp.zeros((), jnp.float32))
        (query_grad, slope_grad), (key_grad, value_grad) = lax.scan(visit, initial, jnp.arange(blocks, dtype=jnp.int32))
        return (query_grad, key_grad.reshape(nodes, HEAD_DIM), value_grad.reshape(nodes, HEAD_DIM), slope_grad)
    query_grad, key_grad, value_grad, d_slopes = lax.map(one_head, (by_heads(query), by_heads(key), by_heads(value), by_heads(d_attn), row_delta, log_norm, slopes))

    def join_heads(array):
        return array.transpose(1, 0, 2).reshape(nodes, HEADS * HEAD_DIM).astype(jnp.bfloat16)
    return (join_heads(query_grad), join_heads(key_grad), join_heads(value_grad), d_out_weight, d_slopes)
```

```python
import functools

import jax
import jax.numpy as jnp
from jax import lax
from jax.experimental import pallas as pl
from jax.experimental.pallas import tpu as pltpu
from jax.sharding import PartitionSpec as P

HEAD_DIM = 64
LOG2E = 1.4426950408889634
f32 = jnp.float32
bf16 = jnp.bfloat16
AXES = ("seq", "head")


def dot(a, b, dims=((1,), (0,))):
    return lax.dot_general(a, b, (dims, ((), ())), preferred_element_type=f32)


def split3(x):
    a = x.astype(bf16).astype(f32)
    r = x - a
    b = r.astype(bf16).astype(f32)
    return a, b, r - b


def prep_query(q, do, sm, aug, qa, doa, q_t, do_t):
    n = q.shape[0]
    rows = []
    for h in range(2):
        rows += list(split3(sm[h : h + 1, :] * (-8.0)))
    for h in range(2):
        rows += list(split3(-sm[2 + h : 3 + h, :]))
    c = [sm[4 + d : 5 + d, :] for d in range(3)]
    rows += c
    rows += list(split3(1.0 + (c[0] * c[0] + c[1] * c[1] + c[2] * c[2])))
    rows += [jnp.ones((1, n), f32)] * 3
    rows += [jnp.zeros((24 - len(rows), n), f32)]
    top = jnp.concatenate(rows, axis=0)
    fill = jnp.zeros((40, n), f32)
    a = jnp.concatenate([top, fill, top, fill], axis=0).T.astype(bf16)
    aug[...] = a
    low = lax.broadcasted_iota(jnp.int32, (n, 128), 1) < HEAD_DIM
    qa[0] = jnp.where(low, q, a)
    qa[1] = jnp.where(low, a, q)
    doa[0] = jnp.where(low, do, a)
    doa[1] = jnp.where(low, a, do)
    q_t[...] = q.T
    do_t[...] = do.T


def prep_key(k, v, cj, ka_t, va_t, ca_t, k_t):
    n = k.shape[0]
    kt = k.T
    vt = v.T
    k_t[...] = kt
    row = lax.broadcasted_iota(jnp.int32, (128, n), 0)
    low = row < HEAD_DIM
    pos = jnp.where(low, row, row - HEAD_DIM)

    def pick(start):
        hit = (pos >= start) & (pos < start + 3)
        return jnp.where(hit, 1.0, 0.0).astype(bf16)

    ka_t[0] = jnp.where(low, kt, pick(0))
    ka_t[1] = jnp.where(low, pick(3), kt)
    va_t[0] = jnp.where(low, vt, pick(6))
    va_t[1] = jnp.where(low, pick(9), vt)
    c = [cj[d : d + 1, :] for d in range(3)]
    m = split3(c[0] * c[0] + c[1] * c[1] + c[2] * c[2])
    ca = jnp.concatenate(
        [jnp.zeros((12, n), f32)]
        + [-2.0 * x for x in c]
        + [jnp.ones((3, n), f32)]
        + list(m)
        + [jnp.zeros((128 - 21, n), f32)],
        axis=0,
    )
    ca_t[...] = ca.astype(bf16)


def tile(qa, doa, aug, q_t, do_t, ka_t, va_t, ca_t, k_t, rates, dq_t, dk_t, dv_t, ds, i, j, bi, bj):
    ii = pl.ds(i, bi)
    jj = pl.ds(j, bj)
    l2 = jnp.maximum(dot(aug[ii, :], ca_t[:, jj]), 1.0)
    lengths = l2 * lax.rsqrt(l2)
    ps = []
    gs = []
    for h in range(2):
        s = dot(qa[h, ii, :], ka_t[h, :, jj])
        gp = dot(doa[h, ii, :], va_t[h, :, jj])
        p = jnp.exp2(s * (LOG2E / 8.0) - lengths * rates[h])
        g = p * gp
        ds[h] += jnp.sum((g * lengths).reshape(bi // 8, 8, bj), axis=0)
        ps.append(p.astype(bf16))
        gs.append(g.astype(bf16))
    for h in range(2):
        hh = pl.ds(h * HEAD_DIM, HEAD_DIM)
        dv_t[hh, jj] += dot(do_t[hh, ii], ps[h])
        dk_t[hh, jj] += dot(q_t[hh, ii], gs[h])
        dq_t[hh, ii] += dot(k_t[hh, jj], gs[h], ((1,), (1,)))


def attend_kernel(
    bi, bj, q, do, sm, k, v, cj,
    dq_out, dk_out, dv_out, ds_out,
    aug, qa, doa, q_t, do_t, ka_t, va_t, ca_t, k_t, dq_t, dk_t, dv_t, ds,
):
    ns, n, _ = q.shape
    dq_t[...] = jnp.zeros_like(dq_t)
    dk_t[...] = jnp.zeros_like(dk_t)
    dv_t[...] = jnp.zeros_like(dv_t)
    ds[...] = jnp.zeros_like(ds)

    def prep(s, _):
        prep_query(
            q[s], do[s], sm[s], aug.at[s], qa.at[s], doa.at[s], q_t.at[s], do_t.at[s]
        )
        prep_key(k[s], v[s], cj[s], ka_t.at[s], va_t.at[s], ca_t.at[s], k_t.at[s])
        return 0

    lax.fori_loop(0, ns, prep, 0)
    rates = [
        jnp.concatenate([sm[0, 7:8, h * 128 : (h + 1) * 128]] * (bj // 128), axis=1) * LOG2E
        for h in range(2)
    ]

    def body(t, _):
        si = t // ns
        sj = t % ns
        nj = n // bj

        def step(u, _):
            i = pl.multiple_of((u // nj) * bi, bi)
            j = pl.multiple_of((u % nj) * bj, bj)
            tile(
                qa.at[si], doa.at[si], aug.at[si], q_t.at[si], do_t.at[si],
                ka_t.at[sj], va_t.at[sj], ca_t.at[sj], k_t.at[sj], rates,
                dq_t.at[si], dk_t.at[sj], dv_t.at[sj], ds, i, j, bi, bj,
            )
            return 0

        lax.fori_loop(0, (n // bi) * nj, step, 0)
        return 0

    lax.fori_loop(0, ns * ns, body, 0)
    dq_out[...] = (dq_t[...] * 0.125).astype(bf16)
    dk_out[...] = (dk_t[...] * 0.125).astype(bf16)
    dv_out[...] = dv_t[...].astype(bf16)
    for h in range(2):
        total = jnp.sum(ds[h], axis=0, keepdims=True)
        total = jnp.sum(total, axis=1, keepdims=True)
        ds_out[h : h + 1, :] = jnp.broadcast_to(-total, (1, 128))


def attend(q, do, sm, k, v, cj, bi, bj):
    ns, n, _ = q.shape
    vm = pl.BlockSpec(memory_space=pltpu.VMEM)

    def wide(*lead):
        return pltpu.VMEM(lead + (n, 128), bf16)

    def tall(dtype, *lead):
        return pltpu.VMEM(lead + (128, n), dtype)

    return pl.pallas_call(
        functools.partial(attend_kernel, bi, bj),
        out_shape=[jax.ShapeDtypeStruct((ns, 128, n), bf16)] * 3
        + [jax.ShapeDtypeStruct((2, 128), f32)],
        in_specs=[vm] * 6,
        out_specs=[vm] * 4,
        scratch_shapes=[
            wide(ns), wide(ns, 2), wide(ns, 2), tall(bf16, ns), tall(bf16, ns),
            tall(bf16, ns, 2), tall(bf16, ns, 2), tall(bf16, ns), tall(bf16, ns),
            tall(f32, ns), tall(f32, ns), tall(f32, ns), pltpu.VMEM((2, 8, bj), f32),
        ],
        compiler_params=pltpu.CompilerParams(vmem_limit_bytes=60 << 20),
        name="attend",
    )(q, do, sm, k, v, cj)


def devices():
    for y in range(4):
        for z in range(4):
            for xh in range(2):
                for xl in range(2):
                    for c in range(2):
                        yield y, z, xh, xl, c


def number(y, z, xh, xl, c):
    return ((y % 4 * 4 + z % 4) * 2 + xh) * 4 + xl * 2 + c


def permute(x, move):
    return lax.ppermute(x, AXES, [(number(*d), number(*move(*d))) for d in devices()])


def cross_a(x):
    return permute(x, lambda y, z, xh, xl, c: (y, z, xh, 1 - xl, c))


def cross_b(x):
    return permute(x, lambda y, z, xh, xl, c: (y, z, 1 - xh, 1 - xl, c))


def along_z(x, s):
    return permute(x, lambda y, z, xh, xl, c: (y, z + s, xh, xl, c))


def along_y(x, s):
    return permute(x, lambda y, z, xh, xl, c: (y + s, z, xh, xl, c))


def exchange(x, xh, axis):
    near = cross_a(lax.dynamic_index_in_dim(x, xh, 0, False))
    far = cross_b(lax.dynamic_index_in_dim(x, 1 - xh, 0, False))
    return jnp.concatenate([near, far], axis=axis)


def give_back(x, xh, rows):
    near = cross_a(x[:, :rows])
    far = cross_b(x[:, rows:])
    first = jnp.where(xh == 0, near, far)
    second = jnp.where(xh == 0, far, near)
    return jnp.concatenate([first, second], axis=0).T


def spread(x, shift):
    return jnp.stack([x] + [shift(x, s) for s in (1, 2, 3)])


def collect(parts, shift):
    total = parts[0].astype(f32)
    for s in (1, 2, 3):
        total = total + shift(parts[s], -s).astype(f32)
    return total.astype(bf16)


def per_device(query, key, value, attn_out, log_norm, d_output, out_weight, coords, slopes):
    rows, cols = query.shape
    groups = cols // HEAD_DIM
    seq = lax.axis_index("seq")
    head = lax.axis_index("head")
    xh = seq % 2

    def pairs(x):
        return x.reshape(rows, 2, 128).transpose(1, 0, 2)

    k = spread(exchange(pairs(key), xh, 0), along_y)
    v = spread(exchange(pairs(value), xh, 0), along_y)
    q = spread(exchange(pairs(query), xh, 0), along_z)

    piece = lax.all_gather(d_output, "head", axis=1, tiled=True)
    d_attn = dot(piece, out_weight, ((1,), (1,))).astype(bf16)
    delta = jnp.sum(
        (d_attn.astype(f32) * attn_out.astype(f32)).reshape(rows, groups, HEAD_DIM), axis=2
    ).T
    do = spread(exchange(pairs(d_attn), xh, 0), along_z)
    pos = coords.astype(f32)
    rates = slopes.reshape(2, 2)
    rate_row = jnp.concatenate(
        [jnp.broadcast_to(rates[:, h : h + 1], (2, 128)) for h in range(2)]
        + [jnp.zeros((2, rows - 256), f32)],
        axis=1,
    )
    small = jnp.concatenate(
        [
            log_norm.reshape(2, 2, rows),
            delta.reshape(2, 2, rows),
            jnp.broadcast_to(pos[None], (2, 3, rows)),
            rate_row[:, None],
        ],
        axis=1,
    )
    small = exchange(small, xh, 1)
    sm = spread(small, along_z)
    cj = spread(small[4:], along_y)
    dq, dk, dv, ds = attend(q, do, sm, k, v, jnp.concatenate([cj, cj], axis=1), 768, 768)
    d_query = give_back(collect(dq, along_z), xh, rows)
    d_key = give_back(collect(dk, along_y), xh, rows)
    d_value = give_back(collect(dv, along_y), xh, rows)

    weight_part = dot(attn_out, piece, ((0,), (0,)))
    weight_sum = lax.psum(weight_part, "seq")
    first = (head ^ 2) * 4 + xh * 2
    place = jnp.arange(16)
    mine = jnp.where(place == first, ds[0, 0], 0.0) + jnp.where(place == first + 1, ds[1, 0], 0.0)
    slope_sum = lax.psum(mine, AXES)
    slope_sum = lax.dynamic_slice_in_dim(slope_sum, head * groups, groups)
    return (d_query, d_key, d_value, weight_sum, slope_sum)


def solution(mesh):
    placed = (
        P("seq", "head"),
        P("seq", "head"),
        P("seq", "head"),
        P("seq", "head"),
        P("head", "seq"),
        P("seq", "head"),
        P("head", None),
        P(None, "seq"),
        P("head"),
    )
    return jax.shard_map(
        per_device,
        mesh=mesh,
        in_specs=placed,
        out_specs=(
            P("seq", "head"),
            P("seq", "head"),
            P("seq", "head"),
            P("head", None),
            P("head"),
        ),
        check_vma=False,
    )
```

```python
import functools

import jax
import jax.numpy as jnp
from jax import lax
from jax.experimental import pallas as pl
from jax.experimental.pallas import tpu as pltpu
from jax.sharding import PartitionSpec as P

HEAD_DIM = 64
LOG2E = 1.4426950408889634
f32 = jnp.float32
bf16 = jnp.bfloat16
AXES = ("seq", "head")


def dot(a, b, dims=((1,), (0,))):
    return lax.dot_general(a, b, (dims, ((), ())), preferred_element_type=f32)


def split3(x):
    a = x.astype(bf16).astype(f32)
    r = x - a
    b = r.astype(bf16).astype(f32)
    return a, b, r - b


def prep_query(q, do, sm, aug, qa, doa, q_t, do_t):
    n = q.shape[0]
    rows = []
    for h in range(2):
        rows += list(split3(sm[h : h + 1, :] * (-8.0)))
    for h in range(2):
        rows += list(split3(-sm[2 + h : 3 + h, :]))
    c = [sm[4 + d : 5 + d, :] for d in range(3)]
    rows += c
    rows += list(split3(1.0 + (c[0] * c[0] + c[1] * c[1] + c[2] * c[2])))
    rows += [jnp.ones((1, n), f32)] * 3
    rows += [jnp.zeros((24 - len(rows), n), f32)]
    top = jnp.concatenate(rows, axis=0)
    fill = jnp.zeros((40, n), f32)
    a = jnp.concatenate([top, fill, top, fill], axis=0).T.astype(bf16)
    aug[...] = a
    low = lax.broadcasted_iota(jnp.int32, (n, 128), 1) < HEAD_DIM
    qa[0] = jnp.where(low, q, a)
    qa[1] = jnp.where(low, a, q)
    doa[0] = jnp.where(low, do, a)
    doa[1] = jnp.where(low, a, do)
    q_t[...] = q.T
    do_t[...] = do.T


def prep_key(k, v, cj, ka_t, va_t, ca_t, k_t):
    n = k.shape[0]
    kt = k.T
    vt = v.T
    k_t[...] = kt
    row = lax.broadcasted_iota(jnp.int32, (128, n), 0)
    low = row < HEAD_DIM
    pos = jnp.where(low, row, row - HEAD_DIM)

    def pick(start):
        hit = (pos >= start) & (pos < start + 3)
        return jnp.where(hit, 1.0, 0.0).astype(bf16)

    ka_t[0] = jnp.where(low, kt, pick(0))
    ka_t[1] = jnp.where(low, pick(3), kt)
    va_t[0] = jnp.where(low, vt, pick(6))
    va_t[1] = jnp.where(low, pick(9), vt)
    c = [cj[d : d + 1, :] for d in range(3)]
    m = split3(c[0] * c[0] + c[1] * c[1] + c[2] * c[2])
    ca = jnp.concatenate(
        [jnp.zeros((12, n), f32)]
        + [-2.0 * x for x in c]
        + [jnp.ones((3, n), f32)]
        + list(m)
        + [jnp.zeros((128 - 21, n), f32)],
        axis=0,
    )
    ca_t[...] = ca.astype(bf16)


def tile(qa, doa, aug, q_t, do_t, ka_t, va_t, ca_t, k_t, rates, dq_t, dk_t, dv_t, ds, i, j, bi, bj):
    ii = pl.ds(i, bi)
    jj = pl.ds(j, bj)
    l2 = jnp.maximum(dot(aug[ii, :], ca_t[:, jj]), 1.0)
    lengths = l2 * lax.rsqrt(l2)
    ps = []
    gs = []
    for h in range(2):
        s = dot(qa[h, ii, :], ka_t[h, :, jj])
        gp = dot(doa[h, ii, :], va_t[h, :, jj])
        p = jnp.exp2(s * (LOG2E / 8.0) - lengths * rates[h])
        g = p * gp
        ds[h] += jnp.sum((g * lengths).reshape(bi // 8, 8, bj), axis=0)
        ps.append(p.astype(bf16))
        gs.append(g.astype(bf16))
    for h in range(2):
        hh = pl.ds(h * HEAD_DIM, HEAD_DIM)
        dv_t[hh, jj] += dot(do_t[hh, ii], ps[h])
        dk_t[hh, jj] += dot(q_t[hh, ii], gs[h])
        dq_t[hh, ii] += dot(k_t[hh, jj], gs[h], ((1,), (1,)))


ORDER = [(q, k) for k in (1, 3, 2) for q in (0, 1, 3, 2)] + [(2, 0), (1, 0), (3, 0), (0, 0)]


def pick_at(t, values):
    out = jnp.int32(values[-1])
    for i in range(len(values) - 2, -1, -1):
        out = jnp.where(t <= i, jnp.int32(values[i]), out)
    return out


def place():
    seq = lax.axis_index("seq")
    head = lax.axis_index("head")
    return seq // 8, (seq // 2) % 4, seq % 2, head // 2, head % 2


def whole_kernel(
    query, key, value, attn_out, log_norm, d_output, out_weight, coords, slopes,
    d_query, d_key, d_value, d_weight, d_slopes,
    piece, qs, dos, sm, kv, cj, sm_src, pair_src, w_part, w_send, w_in, w_sum, w_z, w_x, w_all,
    aug, qa, doa, q_t, do_t, ka_t, va_t, ca_t, k_t, dq_t, dk_t, dv_t, ds,
    dq_send, dq_in, dkv_send, dkv_in, back_send, back_in, ds_send, ds_in,
    send_sem, recv_sem,
):
    rows = query.shape[0]
    n = 2 * rows
    y, z, xh, xl, c = place()
    head = xl * 2 + c

    def at(y, z, xh, xl, c):
        return ((y * 4 + z) * 2 + xh, xl * 2 + c)

    twin = at(y, z, xh, xl, 1 - c)
    near = at(y, z, xh, 1 - xl, c)
    far = at(y, z, 1 - xh, 1 - xl, c)
    across = at(y, z, 1 - xh, xl, c)

    def on_z(s):
        return at(y, (z + s) % 4, xh, xl, c)

    def on_y(s):
        return at((y + s) % 4, z, xh, xl, c)

    partners = [twin, near, far, across] + [on_z(s) for s in (1, 2, 3)] + [on_y(s) for s in (1, 2, 3)]
    barrier = pltpu.get_barrier_semaphore()
    for device in partners:
        pl.semaphore_signal(barrier, inc=1, device_id=device, device_id_type=pl.DeviceIdType.MESH)

    lane = lax.broadcasted_iota(jnp.int32, (1, rows), 1)
    pos = coords[...].astype(f32)
    for p in range(2):
        rate = jnp.where(lane < 128, slopes[2 * p], slopes[2 * p + 1])
        sm_src[p] = jnp.concatenate(
            [log_norm[2 * p : 2 * p + 2, :], jnp.zeros((2, rows), f32), pos, rate], axis=0
        )
    place_rows = jnp.concatenate([pos, jnp.zeros((5, rows), f32)], axis=0)
    cj[0, :, :rows] = place_rows
    cj[4, :, :rows] = place_rows
    piece[head] = d_output[...]
    pl.semaphore_wait(barrier, len(partners))

    count = [0]

    def link(src, dst, device):
        i = count[0]
        count[0] += 1
        return lambda: pltpu.make_async_remote_copy(
            src_ref=src,
            dst_ref=dst,
            send_sem=send_sem.at[i],
            recv_sem=recv_sem.at[i],
            device_id=device,
            device_id_type=pl.DeviceIdType.MESH,
        )

    def start(links):
        for one in links:
            one().start()

    def received(links):
        for one in links:
            one().wait_recv()

    first = pl.ds(0, rows)
    second = pl.ds(rows, rows)
    mine = pl.ds(pl.multiple_of(xh * 128, 128), 128)
    other = pl.ds(pl.multiple_of((1 - xh) * 128, 128), 128)

    own_out = [link(piece.at[head], piece.at[head], near), link(piece.at[head], piece.at[head], twin)]
    near_head = (1 - xl) * 2 + c
    forward = [link(piece.at[near_head], piece.at[near_head], twin)]
    cross_kv = []
    for i, array in enumerate((key, value)):
        cross_kv += [
            link(array.at[:, mine], kv.at[0, i, first], near),
            link(array.at[:, other], kv.at[0, i, second], far),
        ]
    cross_kv += [link(cj.at[4, :, first], cj.at[0, :, second], far)]
    cross_q = [
        link(query.at[:, mine], qs.at[0, first], near),
        link(query.at[:, other], qs.at[0, second], far),
    ]
    cross_do = [
        link(pair_src.at[xh], dos.at[0, first], near),
        link(pair_src.at[1 - xh], dos.at[0, second], far),
        link(sm_src.at[xh], sm.at[0, :, first], near),
        link(sm_src.at[1 - xh], sm.at[0, :, second], far),
    ]
    gather_kv = {
        s: [link(kv.at[0], kv.at[s], on_y(s)), link(cj.at[0], cj.at[s], on_y(s))] for s in (1, 3, 2)
    }
    gather_q = {s: [link(qs.at[0], qs.at[s], on_z(s))] for s in (1, 3, 2)}
    gather_do = {
        s: [link(dos.at[0], dos.at[s], on_z(s)), link(sm.at[0], sm.at[s], on_z(s))] for s in (1, 3, 2)
    }
    give_q = {s: [link(dq_send.at[s], dq_in.at[s], on_z(4 - s))] for s in (1, 3, 2)}
    give_kv = {s: [link(dkv_send.at[s], dkv_in.at[s], on_y(4 - s))] for s in (1, 3, 2)}
    w_rs_y = [link(w_send.at[(y + s) % 4], w_in.at[s], on_y(s)) for s in (1, 3, 2)]
    w_rs_z = [link(w_sum.at[(z + s) % 4], w_z.at[s], on_z(s)) for s in (1, 3, 2)]
    w_rs_x = [link(w_x.at[0], w_x.at[1], across)]
    w_ag_z = [link(w_all.at[y, z], w_all.at[y, z], on_z(s)) for s in (1, 3, 2)]
    w_ag_y = [link(w_all.at[y], w_all.at[y], on_y(s)) for s in (1, 3, 2)]
    back = [
        [
            link(back_send.at[i, :, first], back_in.at[i, xh], near),
            link(back_send.at[i, :, second], back_in.at[i, xh], far),
        ]
        for i in range(3)
    ]
    ds_z = [link(ds_send.at[0], ds_in.at[0, s], on_z(s)) for s in (1, 3, 2)]
    ds_y = [link(ds_send.at[1], ds_in.at[1, s], on_y(s)) for s in (1, 3, 2)]
    ds_x = [
        link(ds_send.at[2], ds_in.at[2, xh], near),
        link(ds_send.at[2], ds_in.at[2, xh], far),
    ]

    start(own_out)
    start(cross_kv)
    start(cross_q)
    dq_t[...] = jnp.zeros_like(dq_t)
    dk_t[...] = jnp.zeros_like(dk_t)
    dv_t[...] = jnp.zeros_like(dv_t)
    ds[...] = jnp.zeros_like(ds)
    received(own_out[:1])
    start(forward)
    received(own_out[1:])
    received(forward)
    total = jnp.zeros((rows, 256), f32)
    for g in range(4):
        total = total + dot(piece[g], out_weight[:, g * 256 : (g + 1) * 256], ((1,), (1,)))
    d_attn = total.astype(bf16)
    product = (d_attn.astype(f32) * attn_out[...].astype(f32)).T
    for p in range(2):
        pair_src[p] = d_attn[:, p * 128 : (p + 1) * 128]
        for h in range(2):
            r = (2 * p + h) * HEAD_DIM
            sm_src[p, 2 + h : 3 + h, :] = jnp.sum(product[r : r + HEAD_DIM], axis=0, keepdims=True)
    start(cross_do)
    received(cross_kv)
    for s in (1, 3, 2):
        start(gather_kv[s])
    received(cross_q)
    for s in (1, 3, 2):
        start(gather_q[s])
    a_t = attn_out[...].T
    for g in range(4):
        part = dot(a_t, piece[g])
        for i in range(4):
            w_part[i, :, g * 256 : (g + 1) * 256] = part[i * 64 : (i + 1) * 64]
    w_send[...] = w_part[...].astype(bf16).reshape(w_send.shape)
    received(cross_do)
    for s in (1, 3, 2):
        start(gather_do[s])

    def prepare_query(s):
        prep_query(
            qs[s], dos[s], sm[s], aug.at[s], qa.at[s], doa.at[s], q_t.at[s], do_t.at[s]
        )

    def prepare_key(s):
        prep_key(kv[s, 0], kv[s, 1], cj[s], ka_t.at[s], va_t.at[s], ca_t.at[s], k_t.at[s])

    prepare_query(0)
    prepare_key(0)
    rates = [
        jnp.concatenate([sm[0, 7:8, h * 128 : (h + 1) * 128]] * (n // 128), axis=1) * LOG2E
        for h in range(2)
    ]

    def take_key(s):
        received(gather_kv[s])
        prepare_key(s)

    def take_query(s):
        received(gather_q[s])
        received(gather_do[s])
        prepare_query(s)

    def send_kv(s):
        dkv_send[s, 0] = dk_t[s].astype(bf16)
        dkv_send[s, 1] = dv_t[s].astype(bf16)
        start(give_kv[s])

    def send_q(s):
        dq_send[s] = dq_t[s].astype(bf16)
        start(give_q[s])

    def weight_y():
        received(w_rs_y)
        total = w_part[y].reshape(w_sum.shape)
        for s in (1, 2, 3):
            total = total + w_in[s].astype(f32)
        w_sum[...] = total
        start(w_rs_z)

    def weight_z():
        received(w_rs_z)
        w_x[0] = w_sum[z] + w_z[1] + w_z[2] + w_z[3]
        start(w_rs_x)

    def weight_x():
        received(w_rs_x)
        w_all[y, z] = (w_x[0] + w_x[1]).astype(bf16)
        start(w_ag_z)

    def weight_gather():
        received(w_ag_z)
        start(w_ag_y)

    def weight_end():
        received(w_ag_y)
        d_weight[...] = w_all[...].astype(f32).reshape(d_weight.shape)

    def add_kv():
        for s in (1, 2, 3):
            received(give_kv[s])
            dk_t[0] += dkv_in[s, 0].astype(f32)
            dv_t[0] += dkv_in[s, 1].astype(f32)

    def add_q(s):
        received(give_q[s])
        dq_t[0] += dq_in[s].astype(f32)

    before = {
        0: [lambda: take_key(1)],
        1: [lambda: take_query(1)],
        2: [lambda: take_query(3)],
        3: [lambda: take_query(2)],
        4: [lambda: send_kv(1), lambda: take_key(3), lambda: start(w_rs_y)],
        6: [weight_y],
        8: [lambda: send_kv(3), lambda: take_key(2), weight_z],
        9: [weight_x],
        10: [weight_gather],
        12: [lambda: send_kv(2)],
        13: [lambda: send_q(2), weight_end],
        14: [lambda: send_q(1)],
        15: [lambda: send_q(3), add_kv, lambda: add_q(2)],
    }

    def block(t, _):
        for step, events in before.items():

            @pl.when(t == step)
            def _(events=events):
                for event in events:
                    event()

        si = pick_at(t, [q for q, _ in ORDER])
        sj = pick_at(t, [k for _, k in ORDER])
        tile(
            qa.at[si], doa.at[si], aug.at[si], q_t.at[si], do_t.at[si],
            ka_t.at[sj], va_t.at[sj], ca_t.at[sj], k_t.at[sj], rates,
            dq_t.at[si], dk_t.at[sj], dv_t.at[sj], ds, 0, 0, n, n,
        )
        return 0

    lax.fori_loop(0, len(ORDER), block, 0)

    rates_sum = [
        jnp.sum(jnp.sum(-ds[h], axis=0, keepdims=True), axis=1, keepdims=True) for h in range(2)
    ]
    ds_send[0] = jnp.concatenate(
        [jnp.broadcast_to(r, (1, 128)) for r in rates_sum] + [jnp.zeros((6, 128), f32)], axis=0
    )
    start(ds_z)
    back_send[2] = dv_t[0].astype(bf16)
    start(back[2])
    back_send[1] = (dk_t[0] * 0.125).astype(bf16)
    start(back[1])
    received(ds_z)
    ds_send[1] = ds_send[0] + ds_in[0, 1] + ds_in[0, 2] + ds_in[0, 3]
    start(ds_y)
    add_q(1)
    add_q(3)
    back_send[0] = (dq_t[0] * 0.125).astype(bf16)
    start(back[0])
    received(ds_y)
    ds_send[2] = ds_send[1] + ds_in[1, 1] + ds_in[1, 2] + ds_in[1, 3]
    start(ds_x)
    for i, out in ((2, d_value), (1, d_key), (0, d_query)):
        received(back[i])
        for p in range(2):
            out[:, p * 128 : (p + 1) * 128] = back_in[i, p].T
    received(ds_x)
    d_slopes[...] = jnp.concatenate([ds_in[2, 0, 0:2], ds_in[2, 1, 0:2]], axis=0)

    sent = [own_out, forward, cross_kv, cross_q, cross_do, w_rs_y, w_rs_z, w_rs_x, w_ag_z, w_ag_y]
    sent += [group[s] for group in (gather_kv, gather_q, gather_do, give_q, give_kv) for s in (1, 2, 3)]
    sent += back + [ds_z, ds_y, ds_x]
    for links in sent:
        for one in links:
            one().wait_send()


LINKS = 62


def per_device(query, key, value, attn_out, log_norm, d_output, out_weight, coords, slopes):
    rows, cols = query.shape
    n = 2 * rows
    vm = pl.BlockSpec(memory_space=pltpu.VMEM)
    quarter = out_weight.shape[0] // 4

    def wide(*lead):
        return pltpu.VMEM(lead + (n, 128), bf16)

    def tall(dtype, *lead):
        return pltpu.VMEM(lead + (128, n), dtype)

    width = out_weight.shape[1]
    scratch = [
        pltpu.VMEM((4, rows, cols), bf16),
        wide(4), wide(4),
        pltpu.VMEM((4, 8, n), f32),
        wide(4, 2),
        pltpu.VMEM((5, 8, n), f32),
        pltpu.VMEM((2, 8, rows), f32),
        pltpu.VMEM((2, rows, 128), bf16),
        pltpu.VMEM((4, quarter, width), f32),
        pltpu.VMEM((4, 4, quarter // 4, width), bf16),
        pltpu.VMEM((4, 4, quarter // 4, width), bf16),
        pltpu.VMEM((4, quarter // 4, width), f32),
        pltpu.VMEM((4, quarter // 4, width), f32),
        pltpu.VMEM((2, quarter // 4, width), f32),
        pltpu.VMEM((4, 4, quarter // 4, width), bf16),
        wide(4), wide(4, 2), wide(4, 2), tall(bf16, 4), tall(bf16, 4),
        tall(bf16, 4, 2), tall(bf16, 4, 2), tall(bf16, 4), tall(bf16, 4),
        tall(f32, 4), tall(f32, 4), tall(f32, 4), pltpu.VMEM((2, 8, n), f32),
        tall(bf16, 4), tall(bf16, 4),
        tall(bf16, 4, 2), tall(bf16, 4, 2),
        tall(bf16, 3), pltpu.VMEM((3, 2, 128, rows), bf16),
        pltpu.VMEM((3, 8, 128), f32), pltpu.VMEM((3, 4, 8, 128), f32),
        pltpu.SemaphoreType.DMA((LINKS,)), pltpu.SemaphoreType.DMA((LINKS,)),
    ]
    d_query, d_key, d_value, d_weight, d_slopes = pl.pallas_call(
        whole_kernel,
        out_shape=[jax.ShapeDtypeStruct((rows, cols), bf16)] * 3
        + [jax.ShapeDtypeStruct(out_weight.shape, f32), jax.ShapeDtypeStruct((4, 128), f32)],
        in_specs=[vm] * 8 + [pl.BlockSpec(memory_space=pltpu.SMEM)],
        out_specs=[vm] * 5,
        scratch_shapes=scratch,
        compiler_params=pltpu.CompilerParams(
            collective_id=0, has_side_effects=True, vmem_limit_bytes=60 << 20
        ),
        name="whole",
    )(query, key, value, attn_out, log_norm, d_output, out_weight, coords, slopes)
    return d_query, d_key, d_value, d_weight, d_slopes[:, 0]


def solution(mesh):
    placed = (
        P("seq", "head"),
        P("seq", "head"),
        P("seq", "head"),
        P("seq", "head"),
        P("head", "seq"),
        P("seq", "head"),
        P("head", None),
        P(None, "seq"),
        P("head"),
    )
    return jax.shard_map(
        per_device,
        mesh=mesh,
        in_specs=placed,
        out_specs=(
            P("seq", "head"),
            P("seq", "head"),
            P("seq", "head"),
            P("head", None),
            P("head"),
        ),
        check_vma=False,
    )
```

```python
import functools

import jax
import jax.numpy as jnp
from jax import lax
from jax.experimental import pallas as pl
from jax.experimental.pallas import tpu as pltpu
from jax.sharding import PartitionSpec as P

HEAD_DIM = 64
LOG2E = 1.4426950408889634
f32 = jnp.float32
bf16 = jnp.bfloat16
AXES = ("seq", "head")


def dot(a, b, dims=((1,), (0,))):
    return lax.dot_general(a, b, (dims, ((), ())), preferred_element_type=f32)


def split3(x):
    a = x.astype(bf16).astype(f32)
    r = x - a
    b = r.astype(bf16).astype(f32)
    return a, b, r - b


def prep_query(q, do, sm, aug, qa, doa, q_t, do_t):
    n = q.shape[0]
    rows = []
    for h in range(2):
        rows += list(split3(sm[h : h + 1, :] * (-8.0)))
    for h in range(2):
        rows += list(split3(-sm[2 + h : 3 + h, :]))
    c = [sm[4 + d : 5 + d, :] for d in range(3)]
    rows += c
    rows += list(split3(1.0 + (c[0] * c[0] + c[1] * c[1] + c[2] * c[2])))
    rows += [jnp.ones((1, n), f32)] * 3
    rows += [jnp.zeros((24 - len(rows), n), f32)]
    top = jnp.concatenate(rows, axis=0)
    fill = jnp.zeros((40, n), f32)
    a = jnp.concatenate([top, fill, top, fill], axis=0).T.astype(bf16)
    aug[...] = a
    low = lax.broadcasted_iota(jnp.int32, (n, 128), 1) < HEAD_DIM
    qa[0] = jnp.where(low, q, a)
    qa[1] = jnp.where(low, a, q)
    doa[0] = jnp.where(low, do, a)
    doa[1] = jnp.where(low, a, do)
    q_t[...] = q.T
    do_t[...] = do.T


def prep_key(k, v, cj, ka_t, va_t, ca_t, k_t):
    n = k.shape[0]
    kt = k.T
    vt = v.T
    k_t[...] = kt
    row = lax.broadcasted_iota(jnp.int32, (128, n), 0)
    low = row < HEAD_DIM
    pos = jnp.where(low, row, row - HEAD_DIM)

    def pick(start):
        hit = (pos >= start) & (pos < start + 3)
        return jnp.where(hit, 1.0, 0.0).astype(bf16)

    ka_t[0] = jnp.where(low, kt, pick(0))
    ka_t[1] = jnp.where(low, pick(3), kt)
    va_t[0] = jnp.where(low, vt, pick(6))
    va_t[1] = jnp.where(low, pick(9), vt)
    c = [cj[d : d + 1, :] for d in range(3)]
    m = split3(c[0] * c[0] + c[1] * c[1] + c[2] * c[2])
    ca = jnp.concatenate(
        [jnp.zeros((12, n), f32)]
        + [-2.0 * x for x in c]
        + [jnp.ones((3, n), f32)]
        + list(m)
        + [jnp.zeros((128 - 21, n), f32)],
        axis=0,
    )
    ca_t[...] = ca.astype(bf16)


CHUNK = 256


def tile(qa, doa, aug, q_t, do_t, ka_t, va_t, ca_t, k_t, rates, dq_t, dk_t, dv_t, ds):
    n = q_t.shape[1]
    pending = []

    def gradients(h, ii, jj, p, g):
        hh = pl.ds(h * HEAD_DIM, HEAD_DIM)
        dv_t[hh, jj] += dot(do_t[hh, ii], p)
        dk_t[hh, jj] += dot(q_t[hh, ii], g)
        dq_t[hh, ii] += dot(k_t[hh, jj], g, ((1,), (1,)))

    for i in range(0, n, CHUNK):
        for j in range(0, n, CHUNK):
            ii = pl.ds(i, CHUNK)
            jj = pl.ds(j, CHUNK)
            l2 = jnp.maximum(dot(aug[ii, :], ca_t[:, jj]), 1.0)
            lengths = l2 * lax.rsqrt(l2)
            for h in range(2):
                s = dot(qa[h, ii, :], ka_t[h, :, jj])
                gp = dot(doa[h, ii, :], va_t[h, :, jj])
                p = jnp.exp2(s * (LOG2E / 8.0) - lengths * rates[h])
                g = p * gp
                ds[h] += jnp.sum((g * lengths).reshape(CHUNK // 8, 8, CHUNK), axis=0)
                pending.append((h, ii, jj, p.astype(bf16), g.astype(bf16)))
                if len(pending) > 1:
                    gradients(*pending.pop(0))
    gradients(*pending.pop(0))


ORDER = [(0, 0)] + [(q, k) for k in (1, 2, 3) for q in (0, 1, 3, 2)] + [(2, 0), (1, 0), (3, 0)]


def pick_at(t, values):
    out = jnp.int32(values[-1])
    for i in range(len(values) - 2, -1, -1):
        out = jnp.where(t <= i, jnp.int32(values[i]), out)
    return out


def place():
    seq = lax.axis_index("seq")
    head = lax.axis_index("head")
    return seq // 8, (seq // 2) % 4, seq % 2, head // 2, head % 2


def whole_kernel(
    query, key, value, attn_out, log_norm, d_output, out_weight, coords, slopes,
    d_query, d_key, d_value, d_weight, d_slopes,
    a_in, o_w, local_sem, piece, qs, dos, sm, kv, cj, sm_src, pair_src, w_part, w_send, w_in, w_sum, w_y, w_x, w_all,
    aug, qa, doa, q_t, do_t, ka_t, va_t, ca_t, k_t, dq_t, dk_t, dv_t, ds,
    dq_send, dq_in, dkv_send, dkv_in, back_send, back_in, ds_send, ds_in,
    send_sem, recv_sem,
):
    rows = query.shape[0]
    n = 2 * rows
    y, z, xh, xl, c = place()
    head = xl * 2 + c

    def at(y, z, xh, xl, c):
        return ((y * 4 + z) * 2 + xh, xl * 2 + c)

    twin = at(y, z, xh, xl, 1 - c)
    near = at(y, z, xh, 1 - xl, c)
    far = at(y, z, 1 - xh, 1 - xl, c)
    across = at(y, z, 1 - xh, xl, c)

    def on_z(s):
        return at(y, (z + s) % 4, xh, xl, c)

    def on_y(s):
        return at((y + s) % 4, z, xh, xl, c)

    partners = [twin, near, far, across] + [on_z(s) for s in (1, 2, 3)] + [on_y(s) for s in (1, 2, 3)]
    barrier = pltpu.get_barrier_semaphore()
    for device in partners:
        pl.semaphore_signal(barrier, inc=1, device_id=device, device_id_type=pl.DeviceIdType.MESH)

    local = [
        pltpu.make_async_copy(src, dst, local_sem.at[i])
        for i, (src, dst) in enumerate(
            ((d_output, piece.at[head]), (out_weight, o_w), (attn_out, a_in))
        )
    ]
    for one in local:
        one.start()
    lane = lax.broadcasted_iota(jnp.int32, (1, rows), 1)
    pos = coords[...].astype(f32)
    for p in range(2):
        rate = jnp.where(lane < 128, slopes[2 * p], slopes[2 * p + 1])
        sm_src[p] = jnp.concatenate(
            [log_norm[2 * p : 2 * p + 2, :], jnp.zeros((2, rows), f32), pos, rate], axis=0
        )
    place_rows = jnp.concatenate([pos, jnp.zeros((5, rows), f32)], axis=0)
    cj[0, :, :rows] = place_rows
    cj[4, :, :rows] = place_rows
    pl.semaphore_wait(barrier, len(partners))

    count = [0]

    def link(src, dst, device):
        i = count[0]
        count[0] += 1
        return lambda: pltpu.make_async_remote_copy(
            src_ref=src,
            dst_ref=dst,
            send_sem=send_sem.at[i],
            recv_sem=recv_sem.at[i],
            device_id=device,
            device_id_type=pl.DeviceIdType.MESH,
        )

    def start(links):
        for one in links:
            one().start()

    def received(links):
        for one in links:
            one().wait_recv()

    first = pl.ds(0, rows)
    second = pl.ds(rows, rows)
    mine = pl.ds(pl.multiple_of(xh * 128, 128), 128)
    other = pl.ds(pl.multiple_of((1 - xh) * 128, 128), 128)

    own_out = [link(d_output, piece.at[head], near), link(d_output, piece.at[head], twin)]
    near_head = (1 - xl) * 2 + c
    forward = [link(piece.at[near_head], piece.at[near_head], twin)]
    near_kv = [
        link(array.at[:, mine], kv.at[0, i, first], near) for i, array in enumerate((key, value))
    ]
    far_kv = [
        link(array.at[:, other], kv.at[0, i, second], far) for i, array in enumerate((key, value))
    ]
    far_kv += [link(cj.at[4, :, first], cj.at[0, :, second], far)]
    near_q = [link(query.at[:, mine], qs.at[0, first], near)]
    far_q = [link(query.at[:, other], qs.at[0, second], far)]
    cross_do = [
        link(pair_src.at[xh], dos.at[0, first], near),
        link(pair_src.at[1 - xh], dos.at[0, second], far),
        link(sm_src.at[xh], sm.at[0, :, first], near),
        link(sm_src.at[1 - xh], sm.at[0, :, second], far),
    ]
    gather_kv = {
        s: [link(kv.at[0], kv.at[s], on_y(s)), link(cj.at[0], cj.at[s], on_y(s))] for s in (1, 3)
    }
    gather_q = {s: [link(qs.at[0], qs.at[s], on_z(s))] for s in (1, 3)}
    gather_do = {
        s: [link(dos.at[0], dos.at[s], on_z(s)), link(sm.at[0], sm.at[s], on_z(s))] for s in (1, 3)
    }
    relay_kv = {
        s: [
            link(kv.at[s, :, half], kv.at[2, :, half], on_y(s)),
            link(cj.at[s, :, half], cj.at[2, :, half], on_y(s)),
        ]
        for s, half in ((1, first), (3, second))
    }
    relay_q = {
        s: [
            link(qs.at[s, half], qs.at[2, half], on_z(s)),
            link(dos.at[s, half], dos.at[2, half], on_z(s)),
            link(sm.at[s, :, half], sm.at[2, :, half], on_z(s)),
        ]
        for s, half in ((1, first), (3, second))
    }
    give_q = {s: [link(dq_send.at[s], dq_in.at[s], on_z(4 - s))] for s in (1, 3, 2)}
    give_kv = {s: [link(dkv_send.at[s], dkv_in.at[s], on_y(4 - s))] for s in (1, 3, 2)}
    w_rs_z = [link(w_send.at[(z + s) % 4], w_in.at[s], on_z(s)) for s in (1, 3, 2)]
    w_rs_y = [link(w_sum.at[(y + s) % 4], w_y.at[s], on_y(s)) for s in (1, 3, 2)]
    w_rs_x = [link(w_x.at[0], w_x.at[1], across)]
    w_ag_y = [link(w_all.at[z, y], w_all.at[z, y], on_y(s)) for s in (1, 3, 2)]
    w_ag_z = [link(w_all.at[z], w_all.at[z], on_z(s)) for s in (1, 3, 2)]
    back = [
        [
            link(back_send.at[i, :, first], back_in.at[i, xh], near),
            link(back_send.at[i, :, second], back_in.at[i, xh], far),
        ]
        for i in range(3)
    ]
    ds_z = [link(ds_send.at[0], ds_in.at[0, s], on_z(s)) for s in (1, 3, 2)]
    ds_y = [link(ds_send.at[1], ds_in.at[1, s], on_y(s)) for s in (1, 3, 2)]
    ds_x = [
        link(ds_send.at[2], ds_in.at[2, xh], near),
        link(ds_send.at[2], ds_in.at[2, xh], far),
    ]

    start(far_kv)
    start(near_kv)
    start(far_q)
    start(own_out[1:])
    for one in near_kv:
        one().wait_send()
    start(own_out[:1])
    dq_t[...] = jnp.zeros_like(dq_t)
    dk_t[...] = jnp.zeros_like(dk_t)
    dv_t[...] = jnp.zeros_like(dv_t)
    ds[...] = jnp.zeros_like(ds)
    received(far_kv)
    received(near_kv)
    for s in (1, 3):
        start(gather_kv[s])
    received(own_out[:1])
    start(forward)
    start(near_q)
    received(own_out[1:])
    received(forward)
    for one in local:
        one.wait()
    total = jnp.zeros((rows, 256), f32)
    for g in range(4):
        total = total + dot(piece[g], o_w[:, g * 256 : (g + 1) * 256], ((1,), (1,)))
    d_attn = total.astype(bf16)
    product = (d_attn.astype(f32) * a_in[...].astype(f32)).T
    for p in range(2):
        pair_src[p] = d_attn[:, p * 128 : (p + 1) * 128]
        for h in range(2):
            r = (2 * p + h) * HEAD_DIM
            sm_src[p, 2 + h : 3 + h, :] = jnp.sum(product[r : r + HEAD_DIM], axis=0, keepdims=True)
    start(cross_do)
    received(far_q)
    received(near_q)
    for s in (1, 3):
        start(gather_q[s])
    a_t = a_in[...].T
    for g in range(4):
        part = dot(a_t, piece[g])
        for i in range(4):
            w_part[i, :, g * 256 : (g + 1) * 256] = part[i * 64 : (i + 1) * 64]
    w_send[...] = w_part[...].astype(bf16).reshape(w_send.shape)
    received(cross_do)
    for s in (1, 3):
        start(gather_do[s])

    def prepare_query(s):
        prep_query(
            qs[s], dos[s], sm[s], aug.at[s], qa.at[s], doa.at[s], q_t.at[s], do_t.at[s]
        )

    def prepare_key(s):
        prep_key(kv[s, 0], kv[s, 1], cj[s], ka_t.at[s], va_t.at[s], ca_t.at[s], k_t.at[s])

    prepare_query(0)
    rates = [
        jnp.concatenate([sm[0, 7:8, h * 128 : (h + 1) * 128]] * (CHUNK // 128), axis=1) * LOG2E
        for h in range(2)
    ]

    def take_key(s):
        received(gather_kv[s])
        start(relay_kv[s])
        prepare_key(s)

    def take_query(s):
        received(gather_q[s])
        received(gather_do[s])
        start(relay_q[s])
        prepare_query(s)

    def relay_key():
        received(gather_kv[3])
        start(relay_kv[3])

    def far_key():
        received(relay_kv[1])
        received(relay_kv[3])
        prepare_key(2)

    def far_query():
        received(relay_q[1])
        received(relay_q[3])
        prepare_query(2)

    def send_kv(s):
        dkv_send[s, 0] = dk_t[s].astype(bf16)
        dkv_send[s, 1] = dv_t[s].astype(bf16)
        start(give_kv[s])

    def send_q(s):
        dq_send[s] = dq_t[s].astype(bf16)
        start(give_q[s])

    def weight_z():
        received(w_rs_z)
        total = w_part[z].reshape(w_sum.shape)
        for s in (1, 2, 3):
            total = total + w_in[s].astype(f32)
        w_sum[...] = total
        start(w_rs_y)

    def weight_y():
        received(w_rs_y)
        w_x[0] = w_sum[y] + w_y[1] + w_y[2] + w_y[3]
        start(w_rs_x)

    def weight_x():
        received(w_rs_x)
        w_all[z, y] = (w_x[0] + w_x[1]).astype(bf16)
        start(w_ag_y)

    def weight_gather():
        received(w_ag_y)
        start(w_ag_z)

    def add_kv():
        for s in (1, 2, 3):
            received(give_kv[s])
            dk_t[0] += dkv_in[s, 0].astype(f32)
            dv_t[0] += dkv_in[s, 1].astype(f32)

    def add_q(s):
        received(give_q[s])
        dq_t[0] += dq_in[s].astype(f32)

    prepare_key(0)
    before = {
        1: [lambda: take_key(1)],
        2: [relay_key, lambda: take_query(1)],
        3: [lambda: take_query(3)],
        4: [far_query, lambda: start(w_rs_z)],
        5: [far_key, lambda: send_kv(1)],
        7: [weight_z],
        9: [lambda: prepare_key(3), weight_y, lambda: send_kv(2)],
        11: [weight_x],
        13: [lambda: send_kv(3), weight_gather],
        14: [lambda: send_q(2)],
        15: [lambda: send_q(1), add_kv],
    }

    def run_events(t, low, high):
        steps = [step for step in before if low <= step < high]
        if high - low == 1:
            for event in before[low]:
                event()
        elif steps:
            middle = (low + high) // 2
            left = any(step < middle for step in steps)
            right = any(step >= middle for step in steps)
            if left and right:
                lax.cond(
                    t < middle,
                    lambda: run_events(t, low, middle),
                    lambda: run_events(t, middle, high),
                )
            elif left:
                pl.when(t < middle)(lambda: run_events(t, low, middle))
            else:
                pl.when(t >= middle)(lambda: run_events(t, middle, high))

    def block(t, _):
        run_events(t, 0, len(ORDER))
        si = pick_at(t, [q for q, _ in ORDER])
        sj = pick_at(t, [k for _, k in ORDER])
        tile(
            qa.at[si], doa.at[si], aug.at[si], q_t.at[si], do_t.at[si],
            ka_t.at[sj], va_t.at[sj], ca_t.at[sj], k_t.at[sj], rates,
            dq_t.at[si], dk_t.at[sj], dv_t.at[sj], ds,
        )
        return 0

    lax.fori_loop(0, len(ORDER), block, 0)
    send_q(3)

    rates_sum = [
        jnp.sum(jnp.sum(-ds[h], axis=0, keepdims=True), axis=1, keepdims=True) for h in range(2)
    ]
    ds_send[0] = jnp.concatenate(
        [jnp.broadcast_to(r, (1, 128)) for r in rates_sum] + [jnp.zeros((6, 128), f32)], axis=0
    )
    start(ds_z)
    back_send[2] = dv_t[0].astype(bf16)
    start(back[2])
    back_send[1] = (dk_t[0] * 0.125).astype(bf16)
    start(back[1])
    received(ds_z)
    ds_send[1] = ds_send[0] + ds_in[0, 1] + ds_in[0, 2] + ds_in[0, 3]
    start(ds_y)
    add_q(2)
    add_q(1)
    add_q(3)
    back_send[0] = (dq_t[0] * 0.125).astype(bf16)
    start(back[0])
    received(ds_y)
    ds_send[2] = ds_send[1] + ds_in[1, 1] + ds_in[1, 2] + ds_in[1, 3]
    start(ds_x)
    for i, out in ((2, d_value), (1, d_key), (0, d_query)):
        received(back[i])
        for p in range(2):
            out[:, p * 128 : (p + 1) * 128] = back_in[i, p].T
    received(w_ag_z)
    d_weight[...] = w_all[...].reshape(d_weight.shape)
    received(ds_x)
    d_slopes[...] = jnp.concatenate([ds_in[2, 0, 0:2], ds_in[2, 1, 0:2]], axis=0)

    sent = [own_out, forward, far_kv, far_q, near_q, cross_do]
    sent += [w_rs_z, w_rs_y, w_rs_x, w_ag_y, w_ag_z]
    sent += [group[s] for group in (give_q, give_kv) for s in (1, 2, 3)]
    groups = (gather_kv, gather_q, gather_do, relay_kv, relay_q)
    sent += [group[s] for group in groups for s in (1, 3)]
    sent += back + [ds_z, ds_y, ds_x]
    for links in sent:
        for one in links:
            one().wait_send()


LINKS = 67


def hand_over(q, k, v, w, s, d_query, d_key, d_value, d_weight, d_slopes):
    d_query[...] = q[...]
    d_key[...] = k[...]
    d_value[...] = v[...]
    d_weight[...] = w[...].astype(f32)
    for i in range(4):
        d_slopes[i] = s[i, 0]


def per_device(query, key, value, attn_out, log_norm, d_output, out_weight, coords, slopes):
    rows, cols = query.shape
    n = 2 * rows
    vm = pl.BlockSpec(memory_space=pltpu.VMEM)
    quarter = out_weight.shape[0] // 4

    def wide(*lead):
        return pltpu.VMEM(lead + (n, 128), bf16)

    def tall(dtype, *lead):
        return pltpu.VMEM(lead + (128, n), dtype)

    width = out_weight.shape[1]
    scratch = [
        pltpu.VMEM((rows, cols), bf16), pltpu.VMEM(out_weight.shape, bf16),
        pltpu.SemaphoreType.DMA((3,)),
        pltpu.VMEM((4, rows, cols), bf16),
        wide(4), wide(4),
        pltpu.VMEM((4, 8, n), f32),
        wide(4, 2),
        pltpu.VMEM((5, 8, n), f32),
        pltpu.VMEM((2, 8, rows), f32),
        pltpu.VMEM((2, rows, 128), bf16),
        pltpu.VMEM((4, quarter, width), f32),
        pltpu.VMEM((4, 4, quarter // 4, width), bf16),
        pltpu.VMEM((4, 4, quarter // 4, width), bf16),
        pltpu.VMEM((4, quarter // 4, width), f32),
        pltpu.VMEM((4, quarter // 4, width), f32),
        pltpu.VMEM((2, quarter // 4, width), f32),
        pltpu.VMEM((4, 4, quarter // 4, width), bf16),
        wide(4), wide(4, 2), wide(4, 2), tall(bf16, 4), tall(bf16, 4),
        tall(bf16, 4, 2), tall(bf16, 4, 2), tall(bf16, 4), tall(bf16, 4),
        tall(f32, 4), tall(f32, 4), tall(f32, 4), pltpu.VMEM((2, 8, CHUNK), f32),
        tall(bf16, 4), tall(bf16, 4),
        tall(bf16, 4, 2), tall(bf16, 4, 2),
        tall(bf16, 3), pltpu.VMEM((3, 2, 128, rows), bf16),
        pltpu.VMEM((3, 8, 128), f32), pltpu.VMEM((3, 4, 8, 128), f32),
        pltpu.SemaphoreType.DMA((LINKS,)), pltpu.SemaphoreType.DMA((LINKS,)),
    ]
    hbm = pl.BlockSpec(memory_space=pl.ANY)
    smem = pl.BlockSpec(memory_space=pltpu.SMEM)
    results = pl.pallas_call(
        whole_kernel,
        out_shape=[jax.ShapeDtypeStruct((rows, cols), bf16)] * 3
        + [jax.ShapeDtypeStruct(out_weight.shape, bf16), jax.ShapeDtypeStruct((4, 128), f32)],
        in_specs=[hbm] * 4 + [vm] + [hbm] * 2 + [vm, smem],
        out_specs=[vm] * 5,
        scratch_shapes=scratch,
        compiler_params=pltpu.CompilerParams(
            collective_id=0, has_side_effects=True, vmem_limit_bytes=60 << 20
        ),
        name="whole",
    )(query, key, value, attn_out, log_norm, d_output, out_weight, coords, slopes)
    return pl.pallas_call(
        hand_over,
        out_shape=[jax.ShapeDtypeStruct((rows, cols), bf16)] * 3
        + [jax.ShapeDtypeStruct(out_weight.shape, f32), jax.ShapeDtypeStruct(slopes.shape, f32)],
        in_specs=[vm] * 4 + [smem],
        out_specs=[vm] * 4 + [smem],
        compiler_params=pltpu.CompilerParams(vmem_limit_bytes=16 << 20),
        name="hand_over",
    )(*results)


def solution(mesh):
    placed = (
        P("seq", "head"),
        P("seq", "head"),
        P("seq", "head"),
        P("seq", "head"),
        P("head", "seq"),
        P("seq", "head"),
        P("head", None),
        P(None, "seq"),
        P("head"),
    )
    return jax.shard_map(
        per_device,
        mesh=mesh,
        in_specs=placed,
        out_specs=(
            P("seq", "head"),
            P("seq", "head"),
            P("seq", "head"),
            P("head", None),
            P("head"),
        ),
        check_vma=False,
    )
```

```python
import functools

import jax
import jax.numpy as jnp
from jax import lax
from jax.experimental import pallas as pl
from jax.experimental.pallas import tpu as pltpu
from jax.sharding import PartitionSpec as P

HEAD_DIM = 64
LOG2E = 1.4426950408889634
f32 = jnp.float32
bf16 = jnp.bfloat16
AXES = ("seq", "head")


def dot(a, b, dims=((1,), (0,))):
    return lax.dot_general(a, b, (dims, ((), ())), preferred_element_type=f32)


def split3(x):
    a = x.astype(bf16).astype(f32)
    r = x - a
    b = r.astype(bf16).astype(f32)
    return a, b, r - b


def prep_query(q, do, sm, aug, qa, doa, q_t, do_t):
    n = q.shape[0]
    rows = []
    for h in range(2):
        rows += list(split3(sm[h : h + 1, :] * (-8.0)))
    for h in range(2):
        rows += list(split3(-sm[2 + h : 3 + h, :]))
    c = [sm[4 + d : 5 + d, :] for d in range(3)]
    rows += c
    rows += list(split3(1.0 + (c[0] * c[0] + c[1] * c[1] + c[2] * c[2])))
    rows += [jnp.ones((1, n), f32)] * 3
    rows += [jnp.zeros((24 - len(rows), n), f32)]
    top = jnp.concatenate(rows, axis=0)
    fill = jnp.zeros((40, n), f32)
    a = jnp.concatenate([top, fill, top, fill], axis=0).T.astype(bf16)
    aug[...] = a
    low = lax.broadcasted_iota(jnp.int32, (n, 128), 1) < HEAD_DIM
    qa[0] = jnp.where(low, q, a)
    qa[1] = jnp.where(low, a, q)
    doa[0] = jnp.where(low, do, a)
    doa[1] = jnp.where(low, a, do)
    q_t[...] = q.T
    do_t[...] = do.T


def prep_key(k, v, cj, ka_t, va_t, ca_t, k_t):
    n = k.shape[0]
    kt = k.T
    vt = v.T
    k_t[...] = kt
    row = lax.broadcasted_iota(jnp.int32, (128, n), 0)
    low = row < HEAD_DIM
    pos = jnp.where(low, row, row - HEAD_DIM)

    def pick(start):
        hit = (pos >= start) & (pos < start + 3)
        return jnp.where(hit, 1.0, 0.0).astype(bf16)

    ka_t[0] = jnp.where(low, kt, pick(0))
    ka_t[1] = jnp.where(low, pick(3), kt)
    va_t[0] = jnp.where(low, vt, pick(6))
    va_t[1] = jnp.where(low, pick(9), vt)
    c = [cj[d : d + 1, :] for d in range(3)]
    m = split3(c[0] * c[0] + c[1] * c[1] + c[2] * c[2])
    ca = jnp.concatenate(
        [jnp.zeros((12, n), f32)]
        + [-2.0 * x for x in c]
        + [jnp.ones((3, n), f32)]
        + list(m)
        + [jnp.zeros((128 - 21, n), f32)],
        axis=0,
    )
    ca_t[...] = ca.astype(bf16)


CHUNK = 256


def tile(qa, doa, aug, q_t, do_t, ka_t, va_t, ca_t, k_t, rates, dq_t, dk_t, dv_t, ds):
    n = q_t.shape[1]
    pending = []

    def gradients(h, ii, jj, p, g):
        hh = pl.ds(h * HEAD_DIM, HEAD_DIM)
        dq_t[hh, ii] += dot(k_t[hh, jj], g, ((1,), (1,)))
        dv_t[hh, jj] += dot(do_t[hh, ii], p)
        dk_t[hh, jj] += dot(q_t[hh, ii], g)

    for i in range(0, n, CHUNK):
        for j in range(0, n, CHUNK):
            ii = pl.ds(i, CHUNK)
            jj = pl.ds(j, CHUNK)
            l2 = dot(aug[ii, :], ca_t[:, jj])
            lengths = l2 * lax.rsqrt(l2)
            for h in range(2):
                s = dot(qa[h, ii, :], ka_t[h, :, jj])
                gp = dot(doa[h, ii, :], va_t[h, :, jj])
                p = jnp.exp2(s * (LOG2E / 8.0) - lengths * rates[h])
                g = p * gp
                ds[h] += jnp.sum((g * lengths).reshape(CHUNK // 8, 8, CHUNK), axis=0)
                pending.append((h, ii, jj, p.astype(bf16), g.astype(bf16)))
                if len(pending) > 1:
                    gradients(*pending.pop(0))
    gradients(*pending.pop(0))


ORDER = [(0, 0), (0, 1), (0, 3), (1, 1), (3, 1), (2, 1)]
ORDER += [(0, 2), (1, 2), (3, 2), (2, 2), (1, 3), (3, 3), (2, 3), (2, 0), (1, 0), (3, 0)]


def pick_at(t, values):
    out = jnp.int32(values[-1])
    for i in range(len(values) - 2, -1, -1):
        out = jnp.where(t <= i, jnp.int32(values[i]), out)
    return out


def place():
    seq = lax.axis_index("seq")
    head = lax.axis_index("head")
    return seq // 8, (seq // 2) % 4, seq % 2, head // 2, head % 2


def whole_kernel(
    query, key, value, attn_out, log_norm, d_output, out_weight, coords, slopes,
    d_query, d_key, d_value, d_weight, d_slopes,
    a_in, o_w, local_sem, piece, qs, dos, sm, kv, cj, sm_src, pair_src, w_part, w_send, w_x, w_sum, w_send_y, w_y, w_sum_y, w_z, w_all,
    aug, qa, doa, q_t, do_t, ka_t, va_t, ca_t, k_t, dq_t, dk_t, dv_t, ds,
    dq_send, dq_in, dkv_send, dkv_in, back_send, back_in, ds_send, ds_in,
    send_sem, recv_sem,
):
    rows = query.shape[0]
    n = 2 * rows
    y, z, xh, xl, c = place()
    head = xl * 2 + c

    def at(y, z, xh, xl, c):
        return ((y * 4 + z) * 2 + xh, xl * 2 + c)

    twin = at(y, z, xh, xl, 1 - c)
    near = at(y, z, xh, 1 - xl, c)
    far = at(y, z, 1 - xh, 1 - xl, c)
    across = at(y, z, 1 - xh, xl, c)

    def on_z(s):
        return at(y, (z + s) % 4, xh, xl, c)

    def on_y(s):
        return at((y + s) % 4, z, xh, xl, c)

    partners = [twin, near, far, across] + [on_z(s) for s in (1, 2, 3)] + [on_y(s) for s in (1, 2, 3)]
    barrier = pltpu.get_barrier_semaphore()
    for device in partners:
        pl.semaphore_signal(barrier, inc=1, device_id=device, device_id_type=pl.DeviceIdType.MESH)

    local = [
        pltpu.make_async_copy(src, dst, local_sem.at[i])
        for i, (src, dst) in enumerate(
            ((d_output, piece.at[head]), (out_weight, o_w), (attn_out, a_in))
        )
    ]
    for one in local:
        one.start()
    lane = lax.broadcasted_iota(jnp.int32, (1, rows), 1)
    pos = coords[...].astype(f32)
    for p in range(2):
        rate = jnp.where(lane < 128, slopes[2 * p], slopes[2 * p + 1])
        sm_src[p] = jnp.concatenate(
            [log_norm[2 * p : 2 * p + 2, :], jnp.zeros((2, rows), f32), pos, rate], axis=0
        )
    place_rows = jnp.concatenate([pos, jnp.zeros((5, rows), f32)], axis=0)
    cj[0, :, :rows] = place_rows
    cj[4, :, :rows] = place_rows
    pl.semaphore_wait(barrier, len(partners))

    count = [0]

    def link(src, dst, device):
        i = count[0]
        count[0] += 1
        return lambda: pltpu.make_async_remote_copy(
            src_ref=src,
            dst_ref=dst,
            send_sem=send_sem.at[i],
            recv_sem=recv_sem.at[i],
            device_id=device,
            device_id_type=pl.DeviceIdType.MESH,
        )

    def start(links):
        for one in links:
            one().start()

    def received(links):
        for one in links:
            one().wait_recv()

    first = pl.ds(0, rows)
    second = pl.ds(rows, rows)
    mine = pl.ds(pl.multiple_of(xh * 128, 128), 128)
    other = pl.ds(pl.multiple_of((1 - xh) * 128, 128), 128)

    own_out = [link(d_output, piece.at[head], near), link(d_output, piece.at[head], twin)]
    near_head = (1 - xl) * 2 + c
    forward = [link(piece.at[near_head], piece.at[near_head], twin)]
    near_kv = [
        link(array.at[:, mine], kv.at[0, i, first], near) for i, array in enumerate((key, value))
    ]
    far_kv = [
        link(array.at[:, other], kv.at[0, i, second], far) for i, array in enumerate((key, value))
    ]
    far_kv += [link(cj.at[4, :, first], cj.at[0, :, second], far)]
    near_q = [link(query.at[:, mine], qs.at[0, first], near)]
    far_q = [link(query.at[:, other], qs.at[0, second], far)]
    cross_do = [
        link(pair_src.at[xh], dos.at[0, first], near),
        link(pair_src.at[1 - xh], dos.at[0, second], far),
        link(sm_src.at[xh], sm.at[0, :, first], near),
        link(sm_src.at[1 - xh], sm.at[0, :, second], far),
    ]
    gather_kv = {
        s: [link(kv.at[0], kv.at[s], on_y(s)), link(cj.at[0], cj.at[s], on_y(s))] for s in (1, 3)
    }
    gather_q = {s: [link(qs.at[0], qs.at[s], on_z(s))] for s in (1, 3)}
    gather_do = {
        s: [link(dos.at[0], dos.at[s], on_z(s)), link(sm.at[0], sm.at[s], on_z(s))] for s in (1, 3)
    }
    relay_kv = {
        s: [
            link(kv.at[s, :, half], kv.at[2, :, half], on_y(s)),
            link(cj.at[s, :, half], cj.at[2, :, half], on_y(s)),
        ]
        for s, half in ((1, first), (3, second))
    }
    relay_q = {
        s: [
            link(qs.at[s, half], qs.at[2, half], on_z(s)),
            link(dos.at[s, half], dos.at[2, half], on_z(s)),
            link(sm.at[s, :, half], sm.at[2, :, half], on_z(s)),
        ]
        for s, half in ((1, first), (3, second))
    }
    give_q = {s: [link(dq_send.at[s], dq_in.at[s], on_z(4 - s))] for s in (1, 3, 2)}
    give_kv = {s: [link(dkv_send.at[s], dkv_in.at[s], on_y(4 - s))] for s in (1, 3, 2)}
    w_rs_x = [link(w_send, w_x, across)]
    w_rs_y = [link(w_send_y.at[(y + s) % 4], w_y.at[s], on_y(s)) for s in (1, 3, 2)]
    w_rs_z = [link(w_sum_y.at[(z + s) % 4], w_z.at[s], on_z(s)) for s in (1, 3, 2)]
    w_ag_z = [link(w_all.at[xh, y, z], w_all.at[xh, y, z], on_z(s)) for s in (1, 3, 2)]
    w_ag_y = [link(w_all.at[xh, y], w_all.at[xh, y], on_y(s)) for s in (1, 3, 2)]
    w_ag_x = [link(w_all.at[xh], w_all.at[xh], across)]
    back = [
        [
            link(back_send.at[i, :, first], back_in.at[i, xh], near),
            link(back_send.at[i, :, second], back_in.at[i, xh], far),
        ]
        for i in range(3)
    ]
    ds_z = [link(ds_send.at[0], ds_in.at[0, s], on_z(s)) for s in (1, 3, 2)]
    ds_y = [link(ds_send.at[1], ds_in.at[1, s], on_y(s)) for s in (1, 3, 2)]
    ds_x = [
        link(ds_send.at[2], ds_in.at[2, xh], near),
        link(ds_send.at[2], ds_in.at[2, xh], far),
    ]

    start(far_kv)
    start(near_kv)
    start(far_q)
    start(own_out[1:])
    for one in near_kv:
        one().wait_send()
    start(own_out[:1])
    dq_t[...] = jnp.zeros_like(dq_t)
    dk_t[...] = jnp.zeros_like(dk_t)
    dv_t[...] = jnp.zeros_like(dv_t)
    ds[...] = jnp.zeros_like(ds)
    received(far_kv)
    received(near_kv)
    for s in (1, 3):
        start(gather_kv[s])
    received(own_out[:1])
    start(forward)
    start(near_q)
    received(own_out[1:])
    received(forward)
    for one in local:
        one.wait()
    total = jnp.zeros((rows, 256), f32)
    for g in range(4):
        total = total + dot(piece[g], o_w[:, g * 256 : (g + 1) * 256], ((1,), (1,)))
    d_attn = total.astype(bf16)
    product = (d_attn.astype(f32) * a_in[...].astype(f32)).T
    for p in range(2):
        pair_src[p] = d_attn[:, p * 128 : (p + 1) * 128]
        for h in range(2):
            r = (2 * p + h) * HEAD_DIM
            sm_src[p, 2 + h : 3 + h, :] = jnp.sum(product[r : r + HEAD_DIM], axis=0, keepdims=True)
    start(cross_do)
    received(far_q)
    received(near_q)
    for s in (1, 3):
        start(gather_q[s])
    a_t = a_in[...].T
    for g in range(4):
        part = dot(a_t, piece[g])
        w_part[g // 2, :, :, :, (g % 2) * 256 : (g % 2 + 1) * 256] = part.reshape(4, 4, 16, 256)
    w_send[...] = w_part[1 - xh].astype(bf16)
    received(cross_do)
    for s in (1, 3):
        start(gather_do[s])
    start(w_rs_x)

    def prepare_query(s):
        prep_query(
            qs[s], dos[s], sm[s], aug.at[s], qa.at[s], doa.at[s], q_t.at[s], do_t.at[s]
        )

    def prepare_key(s):
        prep_key(kv[s, 0], kv[s, 1], cj[s], ka_t.at[s], va_t.at[s], ca_t.at[s], k_t.at[s])

    prepare_query(0)
    rates = [
        jnp.concatenate([sm[0, 7:8, h * 128 : (h + 1) * 128]] * (CHUNK // 128), axis=1) * LOG2E
        for h in range(2)
    ]

    def take_key(s):
        received(gather_kv[s])
        start(relay_kv[s])
        prepare_key(s)

    def take_queries():
        for s in (1, 3):
            received(gather_q[s])
            received(gather_do[s])
            start(relay_q[s])
        prepare_query(1)

    def far_key():
        received(relay_kv[1])
        received(relay_kv[3])
        prepare_key(2)

    def far_query():
        received(relay_q[1])
        received(relay_q[3])
        prepare_query(2)

    def send_kv(s):
        dkv_send[s, 0] = dk_t[s].astype(bf16)
        dkv_send[s, 1] = dv_t[s].astype(bf16)
        start(give_kv[s])

    def send_q(s):
        dq_send[s] = dq_t[s].astype(bf16)
        start(give_q[s])

    def weight_x():
        received(w_rs_x)
        w_sum[...] = w_part[xh] + w_x[...].astype(f32)
        w_send_y[...] = w_sum[...].astype(bf16)
        start(w_rs_y)

    def weight_y():
        received(w_rs_y)
        total = w_sum[y]
        for s in (1, 2, 3):
            total = total + w_y[s].astype(f32)
        w_sum_y[...] = total
        start(w_rs_z)

    def weight_z():
        received(w_rs_z)
        w_all[xh, y, z] = (w_sum_y[z] + w_z[1] + w_z[2] + w_z[3]).astype(bf16)
        start(w_ag_z)

    def weight_gather_y():
        received(w_ag_z)
        start(w_ag_y)

    def weight_gather_x():
        received(w_ag_y)
        start(w_ag_x)

    def add_kv(s):
        received(give_kv[s])
        dk_t[0] += dkv_in[s, 0].astype(f32)
        dv_t[0] += dkv_in[s, 1].astype(f32)

    def add_q(s):
        received(give_q[s])
        dq_t[0] += dq_in[s].astype(f32)

    prepare_key(0)
    before = {
        1: [lambda: take_key(1)],
        2: [lambda: take_key(3)],
        3: [take_queries],
        4: [weight_x, lambda: prepare_query(3)],
        5: [far_query],
        6: [weight_y, lambda: send_kv(1), far_key],
        8: [weight_z],
        10: [weight_gather_y, lambda: send_kv(2)],
        12: [weight_gather_x],
        13: [lambda: send_kv(3)],
        14: [lambda: send_q(2)],
        15: [lambda: send_q(1), lambda: add_kv(1), lambda: add_kv(2)],
    }

    def run_events(t, low, high):
        steps = [step for step in before if low <= step < high]
        if high - low == 1:
            for event in before[low]:
                event()
        elif steps:
            middle = (low + high) // 2
            left = any(step < middle for step in steps)
            right = any(step >= middle for step in steps)
            if left and right:
                lax.cond(
                    t < middle,
                    lambda: run_events(t, low, middle),
                    lambda: run_events(t, middle, high),
                )
            elif left:
                pl.when(t < middle)(lambda: run_events(t, low, middle))
            else:
                pl.when(t >= middle)(lambda: run_events(t, middle, high))

    def block(t, _):
        run_events(t, 0, len(ORDER))
        si = pick_at(t, [q for q, _ in ORDER])
        sj = pick_at(t, [k for _, k in ORDER])
        tile(
            qa.at[si], doa.at[si], aug.at[si], q_t.at[si], do_t.at[si],
            ka_t.at[sj], va_t.at[sj], ca_t.at[sj], k_t.at[sj], rates,
            dq_t.at[si], dk_t.at[sj], dv_t.at[sj], ds,
        )
        return 0

    lax.fori_loop(0, len(ORDER), block, 0)
    send_q(3)

    rates_sum = [
        jnp.sum(jnp.sum(-ds[h], axis=0, keepdims=True), axis=1, keepdims=True) for h in range(2)
    ]
    ds_send[0] = jnp.concatenate(
        [jnp.broadcast_to(r, (1, 128)) for r in rates_sum] + [jnp.zeros((6, 128), f32)], axis=0
    )
    start(ds_z)
    add_kv(3)
    back_send[2] = dv_t[0].astype(bf16)
    start(back[2])
    back_send[1] = (dk_t[0] * 0.125).astype(bf16)
    start(back[1])
    received(ds_z)
    ds_send[1] = ds_send[0] + ds_in[0, 1] + ds_in[0, 2] + ds_in[0, 3]
    start(ds_y)
    add_q(2)
    add_q(1)
    received(ds_y)
    ds_send[2] = ds_send[1] + ds_in[1, 1] + ds_in[1, 2] + ds_in[1, 3]
    start(ds_x)
    add_q(3)
    back_send[0] = (dq_t[0] * 0.125).astype(bf16)
    start(back[0])
    for i, out in ((2, d_value), (1, d_key), (0, d_query)):
        received(back[i])
        for p in range(2):
            out[:, p * 128 : (p + 1) * 128] = back_in[i, p].T
    received(w_ag_x)
    for i in range(2):
        d_weight[:, i * 512 : (i + 1) * 512] = w_all[i].reshape(256, 512)
    received(ds_x)
    d_slopes[...] = jnp.concatenate([ds_in[2, 0, 0:2], ds_in[2, 1, 0:2]], axis=0)

    sent = [own_out, forward, far_kv, far_q, near_q, cross_do]
    sent += [w_rs_x, w_rs_z, w_rs_y, w_ag_y, w_ag_z, w_ag_x]
    sent += [group[s] for group in (give_q, give_kv) for s in (1, 2, 3)]
    groups = (gather_kv, gather_q, gather_do, relay_kv, relay_q)
    sent += [group[s] for group in groups for s in (1, 3)]
    sent += back + [ds_z, ds_y, ds_x]
    for links in sent:
        for one in links:
            one().wait_send()


LINKS = 68


def hand_over(q, k, v, w, s, d_query, d_key, d_value, d_weight, d_slopes):
    d_query[...] = q[...]
    d_key[...] = k[...]
    d_value[...] = v[...]
    d_weight[...] = w[...].astype(f32)
    for i in range(4):
        d_slopes[i] = s[i, 0]


def per_device(query, key, value, attn_out, log_norm, d_output, out_weight, coords, slopes):
    rows, cols = query.shape
    n = 2 * rows
    vm = pl.BlockSpec(memory_space=pltpu.VMEM)
    part = (4, 4, out_weight.shape[0] // 16, out_weight.shape[1] // 2)

    def wide(*lead):
        return pltpu.VMEM(lead + (n, 128), bf16)

    def tall(dtype, *lead):
        return pltpu.VMEM(lead + (128, n), dtype)

    scratch = [
        pltpu.VMEM((rows, cols), bf16), pltpu.VMEM(out_weight.shape, bf16),
        pltpu.SemaphoreType.DMA((3,)),
        pltpu.VMEM((4, rows, cols), bf16),
        wide(4), wide(4),
        pltpu.VMEM((4, 8, n), f32),
        wide(4, 2),
        pltpu.VMEM((5, 8, n), f32),
        pltpu.VMEM((2, 8, rows), f32),
        pltpu.VMEM((2, rows, 128), bf16),
        pltpu.VMEM((2,) + part, f32),
        pltpu.VMEM(part, bf16), pltpu.VMEM(part, bf16),
        pltpu.VMEM(part, f32),
        pltpu.VMEM(part, bf16), pltpu.VMEM(part, bf16),
        pltpu.VMEM(part[1:], f32), pltpu.VMEM(part[1:], f32),
        pltpu.VMEM((2,) + part, bf16),
        wide(4), wide(4, 2), wide(4, 2), tall(bf16, 4), tall(bf16, 4),
        tall(bf16, 4, 2), tall(bf16, 4, 2), tall(bf16, 4), tall(bf16, 4),
        tall(f32, 4), tall(f32, 4), tall(f32, 4), pltpu.VMEM((2, 8, CHUNK), f32),
        tall(bf16, 4), tall(bf16, 4),
        tall(bf16, 4, 2), tall(bf16, 4, 2),
        tall(bf16, 3), pltpu.VMEM((3, 2, 128, rows), bf16),
        pltpu.VMEM((3, 8, 128), f32), pltpu.VMEM((3, 4, 8, 128), f32),
        pltpu.SemaphoreType.DMA((LINKS,)), pltpu.SemaphoreType.DMA((LINKS,)),
    ]
    hbm = pl.BlockSpec(memory_space=pl.ANY)
    smem = pl.BlockSpec(memory_space=pltpu.SMEM)
    results = pl.pallas_call(
        whole_kernel,
        out_shape=[jax.ShapeDtypeStruct((rows, cols), bf16)] * 3
        + [jax.ShapeDtypeStruct(out_weight.shape, bf16), jax.ShapeDtypeStruct((4, 128), f32)],
        in_specs=[hbm] * 4 + [vm] + [hbm] * 2 + [vm, smem],
        out_specs=[vm] * 5,
        scratch_shapes=scratch,
        compiler_params=pltpu.CompilerParams(
            collective_id=0, has_side_effects=True, vmem_limit_bytes=60 << 20
        ),
        name="whole",
    )(query, key, value, attn_out, log_norm, d_output, out_weight, coords, slopes)
    return pl.pallas_call(
        hand_over,
        out_shape=[jax.ShapeDtypeStruct((rows, cols), bf16)] * 3
        + [jax.ShapeDtypeStruct(out_weight.shape, f32), jax.ShapeDtypeStruct(slopes.shape, f32)],
        in_specs=[vm] * 4 + [smem],
        out_specs=[vm] * 4 + [smem],
        compiler_params=pltpu.CompilerParams(vmem_limit_bytes=60 << 20),
        name="hand_over",
    )(*results)


def solution(mesh):
    placed = (
        P("seq", "head"),
        P("seq", "head"),
        P("seq", "head"),
        P("seq", "head"),
        P("head", "seq"),
        P("seq", "head"),
        P("head", None),
        P(None, "seq"),
        P("head"),
    )
    return jax.shard_map(
        per_device,
        mesh=mesh,
        in_specs=placed,
        out_specs=(
            P("seq", "head"),
            P("seq", "head"),
            P("seq", "head"),
            P("head", None),
            P("head"),
        ),
        check_vma=False,
    )
```

```python
import functools

import jax
import jax.numpy as jnp
from jax import lax
from jax.experimental import pallas as pl
from jax.experimental.pallas import tpu as pltpu
from jax.sharding import PartitionSpec as P

HEAD_DIM = 64
LOG2E = 1.4426950408889634
f32 = jnp.float32
bf16 = jnp.bfloat16
AXES = ("seq", "head")


def dot(a, b, dims=((1,), (0,))):
    return lax.dot_general(a, b, (dims, ((), ())), preferred_element_type=f32)


def split3(x):
    a = x.astype(bf16).astype(f32)
    r = x - a
    b = r.astype(bf16).astype(f32)
    return a, b, r - b


def prep_query(q, do, sm, aug, qa, doa, q_t, do_t):
    n = q.shape[0]
    rows = []
    for h in range(2):
        rows += list(split3(sm[h : h + 1, :] * (-8.0)))
    for h in range(2):
        rows += list(split3(-sm[2 + h : 3 + h, :]))
    c = [sm[4 + d : 5 + d, :] for d in range(3)]
    rows += c
    rows += list(split3(1.0 + (c[0] * c[0] + c[1] * c[1] + c[2] * c[2])))
    rows += [jnp.ones((1, n), f32)] * 3
    rows += [jnp.zeros((24 - len(rows), n), f32)]
    top = jnp.concatenate(rows, axis=0)
    fill = jnp.zeros((40, n), f32)
    a = jnp.concatenate([top, fill, top, fill], axis=0).T.astype(bf16)
    aug[...] = a
    low = lax.broadcasted_iota(jnp.int32, (n, 128), 1) < HEAD_DIM
    qa[0] = jnp.where(low, q, a)
    qa[1] = jnp.where(low, a, q)
    doa[0] = jnp.where(low, do, a)
    doa[1] = jnp.where(low, a, do)
    q_t[...] = q.T
    do_t[...] = do.T


def prep_key(k, v, cj, ka_t, va_t, ca_t, k_t):
    n = k.shape[0]
    kt = k.T
    vt = v.T
    k_t[...] = kt
    row = lax.broadcasted_iota(jnp.int32, (128, n), 0)
    low = row < HEAD_DIM
    pos = jnp.where(low, row, row - HEAD_DIM)

    def pick(start):
        hit = (pos >= start) & (pos < start + 3)
        return jnp.where(hit, 1.0, 0.0).astype(bf16)

    ka_t[0] = jnp.where(low, kt, pick(0))
    ka_t[1] = jnp.where(low, pick(3), kt)
    va_t[0] = jnp.where(low, vt, pick(6))
    va_t[1] = jnp.where(low, pick(9), vt)
    c = [cj[d : d + 1, :] for d in range(3)]
    m = split3(c[0] * c[0] + c[1] * c[1] + c[2] * c[2])
    ca = jnp.concatenate(
        [jnp.zeros((12, n), f32)]
        + [-2.0 * x for x in c]
        + [jnp.ones((3, n), f32)]
        + list(m)
        + [jnp.zeros((128 - 21, n), f32)],
        axis=0,
    )
    ca_t[...] = ca.astype(bf16)


CHUNK = 256


def tile(parts, ka_t, va_t, ca_t, k_t, dk_t, dv_t, rates, ds):
    n = k_t.shape[1]
    pending = []

    def gradients(part, h, ii, jj, p, g):
        _, _, _, q_t, do_t, dq_t = part
        hh = pl.ds(h * HEAD_DIM, HEAD_DIM)
        dq_t[hh, ii] += dot(k_t[hh, jj], g, ((1,), (1,)))
        dv_t[hh, jj] += dot(do_t[hh, ii], p)
        dk_t[hh, jj] += dot(q_t[hh, ii], g)

    for part in parts:
        qa, doa, aug = part[:3]
        for i in range(0, n, CHUNK):
            for j in range(0, n, CHUNK):
                ii = pl.ds(i, CHUNK)
                jj = pl.ds(j, CHUNK)
                l2 = dot(aug[ii, :], ca_t[:, jj])
                lengths = l2 * lax.rsqrt(l2)
                for h in range(2):
                    s = dot(qa[h, ii, :], ka_t[h, :, jj])
                    gp = dot(doa[h, ii, :], va_t[h, :, jj])
                    p = jnp.exp2(s * (LOG2E / 8.0) - lengths * rates[h])
                    g = p * gp
                    ds[h] += jnp.sum((g * lengths).reshape(CHUNK // 8, 8, CHUNK), axis=0)
                    pending.append((part, h, ii, jj, p.astype(bf16), g.astype(bf16)))
                    if len(pending) > 1:
                        gradients(*pending.pop(0))
    gradients(*pending.pop(0))


START = [((q,), k) for q, k in ((0, 0), (0, 1), (0, 3), (1, 1), (3, 1), (2, 1))]
PAIRS = [((0, 1), 2), ((3, 2), 2), ((1, 3), 3)]
END = [((q,), k) for q, k in ((2, 3), (2, 0), (1, 0), (3, 0))]


def pick_at(t, values):
    out = jnp.int32(values[-1])
    for i in range(len(values) - 2, -1, -1):
        out = jnp.where(t <= i, jnp.int32(values[i]), out)
    return out


def place():
    seq = lax.axis_index("seq")
    head = lax.axis_index("head")
    return seq // 8, (seq // 2) % 4, seq % 2, head // 2, head % 2


def whole_kernel(
    query, key, value, attn_out, log_norm, d_output, out_weight, coords, slopes,
    d_query, d_key, d_value, d_weight, d_slopes,
    a_in, o_w, local_sem, piece, qs, dos, sm, kv, cj, sm_src, pair_src, w_part, w_send, w_x, w_sum, w_send_y, w_y, w_sum_y, w_z, w_all,
    aug, qa, doa, q_t, do_t, ka_t, va_t, ca_t, k_t, dq_t, dk_t, dv_t, ds,
    dq_send, dq_in, dkv_send, dkv_in, back_send, back_in, ds_send, ds_in,
    send_sem, recv_sem,
):
    rows = query.shape[0]
    n = 2 * rows
    y, z, xh, xl, c = place()
    head = xl * 2 + c

    def at(y, z, xh, xl, c):
        return ((y * 4 + z) * 2 + xh, xl * 2 + c)

    twin = at(y, z, xh, xl, 1 - c)
    near = at(y, z, xh, 1 - xl, c)
    far = at(y, z, 1 - xh, 1 - xl, c)
    across = at(y, z, 1 - xh, xl, c)

    def on_z(s):
        return at(y, (z + s) % 4, xh, xl, c)

    def on_y(s):
        return at((y + s) % 4, z, xh, xl, c)

    partners = [twin, near, far, across] + [on_z(s) for s in (1, 2, 3)] + [on_y(s) for s in (1, 2, 3)]
    barrier = pltpu.get_barrier_semaphore()
    for device in partners:
        pl.semaphore_signal(barrier, inc=1, device_id=device, device_id_type=pl.DeviceIdType.MESH)

    local = [
        pltpu.make_async_copy(src, dst, local_sem.at[i])
        for i, (src, dst) in enumerate(
            ((d_output, piece.at[head]), (out_weight, o_w), (attn_out, a_in))
        )
    ]
    for one in local:
        one.start()
    lane = lax.broadcasted_iota(jnp.int32, (1, rows), 1)
    pos = coords[...].astype(f32)
    for p in range(2):
        rate = jnp.where(lane < 128, slopes[2 * p], slopes[2 * p + 1])
        sm_src[p] = jnp.concatenate(
            [log_norm[2 * p : 2 * p + 2, :], jnp.zeros((2, rows), f32), pos, rate], axis=0
        )
    place_rows = jnp.concatenate([pos, jnp.zeros((5, rows), f32)], axis=0)
    cj[0, :, :rows] = place_rows
    cj[4, :, :rows] = place_rows
    pl.semaphore_wait(barrier, len(partners))

    count = [0]

    def link(src, dst, device):
        i = count[0]
        count[0] += 1
        return lambda: pltpu.make_async_remote_copy(
            src_ref=src,
            dst_ref=dst,
            send_sem=send_sem.at[i],
            recv_sem=recv_sem.at[i],
            device_id=device,
            device_id_type=pl.DeviceIdType.MESH,
        )

    def start(links):
        for one in links:
            one().start()

    def received(links):
        for one in links:
            one().wait_recv()

    first = pl.ds(0, rows)
    second = pl.ds(rows, rows)
    mine = pl.ds(pl.multiple_of(xh * 128, 128), 128)
    other = pl.ds(pl.multiple_of((1 - xh) * 128, 128), 128)

    own_out = [link(d_output, piece.at[head], near), link(d_output, piece.at[head], twin)]
    near_head = (1 - xl) * 2 + c
    forward = [link(piece.at[near_head], piece.at[near_head], twin)]
    near_kv = [
        link(array.at[:, mine], kv.at[0, i, first], near) for i, array in enumerate((key, value))
    ]
    far_kv = [
        link(array.at[:, other], kv.at[0, i, second], far) for i, array in enumerate((key, value))
    ]
    far_kv += [link(cj.at[4, :, first], cj.at[0, :, second], far)]
    near_q = [link(query.at[:, mine], qs.at[0, first], near)]
    far_q = [link(query.at[:, other], qs.at[0, second], far)]
    cross_do = [
        link(pair_src.at[xh], dos.at[0, first], near),
        link(pair_src.at[1 - xh], dos.at[0, second], far),
        link(sm_src.at[xh], sm.at[0, :, first], near),
        link(sm_src.at[1 - xh], sm.at[0, :, second], far),
    ]
    gather_kv = {
        s: [link(kv.at[0], kv.at[s], on_y(s)), link(cj.at[0], cj.at[s], on_y(s))] for s in (1, 3)
    }
    gather_q = {s: [link(qs.at[0], qs.at[s], on_z(s))] for s in (1, 3)}
    gather_do = {
        s: [link(dos.at[0], dos.at[s], on_z(s)), link(sm.at[0], sm.at[s], on_z(s))] for s in (1, 3)
    }
    relay_kv = {
        s: [
            link(kv.at[s, :, half], kv.at[2, :, half], on_y(s)),
            link(cj.at[s, :, half], cj.at[2, :, half], on_y(s)),
        ]
        for s, half in ((1, first), (3, second))
    }
    relay_q = {
        s: [
            link(qs.at[s, half], qs.at[2, half], on_z(s)),
            link(dos.at[s, half], dos.at[2, half], on_z(s)),
            link(sm.at[s, :, half], sm.at[2, :, half], on_z(s)),
        ]
        for s, half in ((1, first), (3, second))
    }
    give_q = {s: [link(dq_send.at[s], dq_in.at[s], on_z(4 - s))] for s in (1, 3, 2)}
    give_kv = {s: [link(dkv_send.at[s], dkv_in.at[s], on_y(4 - s))] for s in (1, 3, 2)}
    w_rs_x = [link(w_send, w_x, across)]
    w_rs_y = [link(w_send_y.at[(y + s) % 4], w_y.at[s], on_y(s)) for s in (1, 3, 2)]
    w_rs_z = [link(w_sum_y.at[(z + s) % 4], w_z.at[s], on_z(s)) for s in (1, 3, 2)]
    w_ag_z = [link(w_all.at[xh, y, z], w_all.at[xh, y, z], on_z(s)) for s in (1, 3, 2)]
    w_ag_y = [link(w_all.at[xh, y], w_all.at[xh, y], on_y(s)) for s in (1, 3, 2)]
    w_ag_x = [link(w_all.at[xh], w_all.at[xh], across)]
    back = [
        [
            link(back_send.at[i, :, first], back_in.at[i, xh], near),
            link(back_send.at[i, :, second], back_in.at[i, xh], far),
        ]
        for i in range(3)
    ]
    ds_z = [link(ds_send.at[0], ds_in.at[0, s], on_z(s)) for s in (1, 3, 2)]
    ds_y = [link(ds_send.at[1], ds_in.at[1, s], on_y(s)) for s in (1, 3, 2)]
    ds_x = [
        link(ds_send.at[2], ds_in.at[2, xh], near),
        link(ds_send.at[2], ds_in.at[2, xh], far),
    ]

    start(far_kv)
    start(near_kv)
    start(far_q)
    start(own_out[1:])
    for one in near_kv:
        one().wait_send()
    start(own_out[:1])
    dq_t[...] = jnp.zeros_like(dq_t)
    dk_t[...] = jnp.zeros_like(dk_t)
    dv_t[...] = jnp.zeros_like(dv_t)
    ds[...] = jnp.zeros_like(ds)
    received(far_kv)
    received(near_kv)
    for s in (1, 3):
        start(gather_kv[s])
    received(own_out[:1])
    start(forward)
    start(near_q)
    received(own_out[1:])
    received(forward)
    for one in local:
        one.wait()
    total = jnp.zeros((rows, 256), f32)
    for g in range(4):
        total = total + dot(piece[g], o_w[:, g * 256 : (g + 1) * 256], ((1,), (1,)))
    d_attn = total.astype(bf16)
    product = (d_attn.astype(f32) * a_in[...].astype(f32)).T
    for p in range(2):
        pair_src[p] = d_attn[:, p * 128 : (p + 1) * 128]
        for h in range(2):
            r = (2 * p + h) * HEAD_DIM
            sm_src[p, 2 + h : 3 + h, :] = jnp.sum(product[r : r + HEAD_DIM], axis=0, keepdims=True)
    start(cross_do)
    received(far_q)
    received(near_q)
    for s in (1, 3):
        start(gather_q[s])
    a_t = a_in[...].T
    for g in range(4):
        part = dot(a_t, piece[g])
        w_part[g // 2, :, :, :, (g % 2) * 256 : (g % 2 + 1) * 256] = part.reshape(4, 4, 16, 256)
    w_send[...] = w_part[1 - xh].astype(bf16)
    received(cross_do)
    for s in (1, 3):
        start(gather_do[s])
    start(w_rs_x)

    def prepare_query(s):
        prep_query(
            qs[s], dos[s], sm[s], aug.at[s], qa.at[s], doa.at[s], q_t.at[s], do_t.at[s]
        )

    def prepare_key(s):
        prep_key(kv[s, 0], kv[s, 1], cj[s], ka_t.at[s], va_t.at[s], ca_t.at[s], k_t.at[s])

    prepare_query(0)
    rates = [
        jnp.concatenate([sm[0, 7:8, h * 128 : (h + 1) * 128]] * (CHUNK // 128), axis=1) * LOG2E
        for h in range(2)
    ]

    def take_key(s):
        received(gather_kv[s])
        start(relay_kv[s])
        prepare_key(s)

    def take_queries():
        for s in (1, 3):
            received(gather_q[s])
            received(gather_do[s])
            start(relay_q[s])
        prepare_query(1)

    def far_key():
        received(relay_kv[1])
        received(relay_kv[3])
        prepare_key(2)

    def far_query():
        received(relay_q[1])
        received(relay_q[3])
        prepare_query(2)

    def send_kv(s):
        dkv_send[s, 0] = dk_t[s].astype(bf16)
        dkv_send[s, 1] = dv_t[s].astype(bf16)
        start(give_kv[s])

    def send_q(s):
        dq_send[s] = dq_t[s].astype(bf16)
        start(give_q[s])

    def weight_x():
        received(w_rs_x)
        w_sum[...] = w_part[xh] + w_x[...].astype(f32)
        w_send_y[...] = w_sum[...].astype(bf16)
        start(w_rs_y)

    def weight_y():
        received(w_rs_y)
        total = w_sum[y]
        for s in (1, 2, 3):
            total = total + w_y[s].astype(f32)
        w_sum_y[...] = total
        start(w_rs_z)

    def weight_z():
        received(w_rs_z)
        w_all[xh, y, z] = (w_sum_y[z] + w_z[1] + w_z[2] + w_z[3]).astype(bf16)
        start(w_ag_z)

    def weight_gather_y():
        received(w_ag_z)
        start(w_ag_y)

    def weight_gather_x():
        received(w_ag_y)
        start(w_ag_x)

    def add_kv(s):
        received(give_kv[s])
        dk_t[0] += dkv_in[s, 0].astype(f32)
        dv_t[0] += dkv_in[s, 1].astype(f32)

    def add_q(s):
        received(give_q[s])
        dq_t[0] += dq_in[s].astype(f32)

    prepare_key(0)
    before = {
        1: [lambda: take_key(1)],
        2: [lambda: take_key(3)],
        3: [take_queries],
        4: [weight_x, lambda: prepare_query(3)],
        5: [far_query],
        6: [weight_y, lambda: send_kv(1), far_key],
        8: [weight_z],
        10: [weight_gather_y, lambda: send_kv(2)],
        12: [weight_gather_x],
        13: [lambda: send_kv(3)],
        14: [lambda: send_q(2)],
        15: [lambda: send_q(1), lambda: add_kv(1), lambda: add_kv(2)],
    }

    def run_events(t, steps):
        if len(steps) == 1:
            for event in before.get(steps[0], []):
                event()
        else:
            middle = len(steps) // 2
            lax.cond(
                t < steps[middle],
                lambda: run_events(t, steps[:middle]),
                lambda: run_events(t, steps[middle:]),
            )

    def blocks(order, first_step):
        width = len(order[0][0])
        steps = [first_step + i * width for i in range(len(order))]

        def block(i, _):
            run_events(first_step + i * width, steps)
            sj = pick_at(i, [k for _, k in order])
            parts = []
            for m in range(width):
                si = pick_at(i, [q[m] for q, _ in order])
                parts.append([x.at[si] for x in (qa, doa, aug, q_t, do_t, dq_t)])
            tile(
                parts, ka_t.at[sj], va_t.at[sj], ca_t.at[sj], k_t.at[sj], dk_t.at[sj], dv_t.at[sj],
                rates, ds,
            )
            return 0

        lax.fori_loop(0, len(order), block, 0)
        return first_step + len(order) * width

    step = blocks(START, 0)
    step = blocks(PAIRS, step)
    blocks(END, step)
    send_q(3)

    rates_sum = [
        jnp.sum(jnp.sum(-ds[h], axis=0, keepdims=True), axis=1, keepdims=True) for h in range(2)
    ]
    ds_send[0] = jnp.concatenate(
        [jnp.broadcast_to(r, (1, 128)) for r in rates_sum] + [jnp.zeros((6, 128), f32)], axis=0
    )
    start(ds_z)
    add_kv(3)
    back_send[2] = dv_t[0].astype(bf16)
    start(back[2])
    back_send[1] = (dk_t[0] * 0.125).astype(bf16)
    start(back[1])
    received(ds_z)
    ds_send[1] = ds_send[0] + ds_in[0, 1] + ds_in[0, 2] + ds_in[0, 3]
    start(ds_y)
    add_q(2)
    add_q(1)
    received(ds_y)
    ds_send[2] = ds_send[1] + ds_in[1, 1] + ds_in[1, 2] + ds_in[1, 3]
    start(ds_x)
    add_q(3)
    back_send[0] = (dq_t[0] * 0.125).astype(bf16)
    start(back[0])
    for i, out in ((2, d_value), (1, d_key), (0, d_query)):
        received(back[i])
        for p in range(2):
            out[:, p * 128 : (p + 1) * 128] = back_in[i, p].T
    received(w_ag_x)
    for i in range(2):
        d_weight[:, i * 512 : (i + 1) * 512] = w_all[i].reshape(256, 512)
    received(ds_x)
    d_slopes[...] = jnp.concatenate([ds_in[2, 0, 0:2], ds_in[2, 1, 0:2]], axis=0)

    sent = [own_out, forward, far_kv, far_q, near_q, cross_do]
    sent += [w_rs_x, w_rs_z, w_rs_y, w_ag_y, w_ag_z, w_ag_x]
    sent += [group[s] for group in (give_q, give_kv) for s in (1, 2, 3)]
    groups = (gather_kv, gather_q, gather_do, relay_kv, relay_q)
    sent += [group[s] for group in groups for s in (1, 3)]
    sent += back + [ds_z, ds_y, ds_x]
    for links in sent:
        for one in links:
            one().wait_send()


LINKS = 68


def hand_over(q, k, v, w, s, d_query, d_key, d_value, d_weight, d_slopes):
    d_query[...] = q[...]
    d_key[...] = k[...]
    d_value[...] = v[...]
    d_weight[...] = w[...].astype(f32)
    for i in range(4):
        d_slopes[i] = s[i, 0]


def per_device(query, key, value, attn_out, log_norm, d_output, out_weight, coords, slopes):
    rows, cols = query.shape
    n = 2 * rows
    vm = pl.BlockSpec(memory_space=pltpu.VMEM)
    part = (4, 4, out_weight.shape[0] // 16, out_weight.shape[1] // 2)

    def wide(*lead):
        return pltpu.VMEM(lead + (n, 128), bf16)

    def tall(dtype, *lead):
        return pltpu.VMEM(lead + (128, n), dtype)

    scratch = [
        pltpu.VMEM((rows, cols), bf16), pltpu.VMEM(out_weight.shape, bf16),
        pltpu.SemaphoreType.DMA((3,)),
        pltpu.VMEM((4, rows, cols), bf16),
        wide(4), wide(4),
        pltpu.VMEM((4, 8, n), f32),
        wide(4, 2),
        pltpu.VMEM((5, 8, n), f32),
        pltpu.VMEM((2, 8, rows), f32),
        pltpu.VMEM((2, rows, 128), bf16),
        pltpu.VMEM((2,) + part, f32),
        pltpu.VMEM(part, bf16), pltpu.VMEM(part, bf16),
        pltpu.VMEM(part, f32),
        pltpu.VMEM(part, bf16), pltpu.VMEM(part, bf16),
        pltpu.VMEM(part[1:], f32), pltpu.VMEM(part[1:], f32),
        pltpu.VMEM((2,) + part, bf16),
        wide(4), wide(4, 2), wide(4, 2), tall(bf16, 4), tall(bf16, 4),
        tall(bf16, 4, 2), tall(bf16, 4, 2), tall(bf16, 4), tall(bf16, 4),
        tall(f32, 4), tall(f32, 4), tall(f32, 4), pltpu.VMEM((2, 8, CHUNK), f32),
        tall(bf16, 4), tall(bf16, 4),
        tall(bf16, 4, 2), tall(bf16, 4, 2),
        tall(bf16, 3), pltpu.VMEM((3, 2, 128, rows), bf16),
        pltpu.VMEM((3, 8, 128), f32), pltpu.VMEM((3, 4, 8, 128), f32),
        pltpu.SemaphoreType.DMA((LINKS,)), pltpu.SemaphoreType.DMA((LINKS,)),
    ]
    hbm = pl.BlockSpec(memory_space=pl.ANY)
    smem = pl.BlockSpec(memory_space=pltpu.SMEM)
    results = pl.pallas_call(
        whole_kernel,
        out_shape=[jax.ShapeDtypeStruct((rows, cols), bf16)] * 3
        + [jax.ShapeDtypeStruct(out_weight.shape, bf16), jax.ShapeDtypeStruct((4, 128), f32)],
        in_specs=[hbm] * 4 + [vm] + [hbm] * 2 + [vm, smem],
        out_specs=[vm] * 5,
        scratch_shapes=scratch,
        compiler_params=pltpu.CompilerParams(
            collective_id=0, has_side_effects=True, vmem_limit_bytes=60 << 20
        ),
        name="whole",
    )(query, key, value, attn_out, log_norm, d_output, out_weight, coords, slopes)
    return pl.pallas_call(
        hand_over,
        out_shape=[jax.ShapeDtypeStruct((rows, cols), bf16)] * 3
        + [jax.ShapeDtypeStruct(out_weight.shape, f32), jax.ShapeDtypeStruct(slopes.shape, f32)],
        in_specs=[vm] * 4 + [smem],
        out_specs=[vm] * 4 + [smem],
        compiler_params=pltpu.CompilerParams(vmem_limit_bytes=60 << 20),
        name="hand_over",
    )(*results)


def solution(mesh):
    placed = (
        P("seq", "head"),
        P("seq", "head"),
        P("seq", "head"),
        P("seq", "head"),
        P("head", "seq"),
        P("seq", "head"),
        P("head", None),
        P(None, "seq"),
        P("head"),
    )
    return jax.shard_map(
        per_device,
        mesh=mesh,
        in_specs=placed,
        out_specs=(
            P("seq", "head"),
            P("seq", "head"),
            P("seq", "head"),
            P("head", None),
            P("head"),
        ),
        check_vma=False,
    )
```

```python
import functools

import jax
import jax.numpy as jnp
from jax import lax
from jax.experimental import pallas as pl
from jax.experimental.pallas import tpu as pltpu
from jax.sharding import PartitionSpec as P

HEAD_DIM = 64
LOG2E = 1.4426950408889634
f32 = jnp.float32
bf16 = jnp.bfloat16
AXES = ("seq", "head")


def dot(a, b, dims=((1,), (0,))):
    return lax.dot_general(a, b, (dims, ((), ())), preferred_element_type=f32)


def split3(x):
    a = x.astype(bf16).astype(f32)
    r = x - a
    b = r.astype(bf16).astype(f32)
    return a, b, r - b


def prep_query(q, do, sm, aug, qa, doa, q_t, do_t):
    n = q.shape[0]
    rows = []
    for h in range(2):
        rows += list(split3(sm[h : h + 1, :] * (-8.0)))
    for h in range(2):
        rows += list(split3(-sm[2 + h : 3 + h, :]))
    c = [sm[4 + d : 5 + d, :] for d in range(3)]
    rows += c
    rows += list(split3(1.0 + (c[0] * c[0] + c[1] * c[1] + c[2] * c[2])))
    rows += [jnp.ones((1, n), f32)] * 3
    rows += [jnp.zeros((24 - len(rows), n), f32)]
    top = jnp.concatenate(rows, axis=0)
    fill = jnp.zeros((40, n), f32)
    a = jnp.concatenate([top, fill, top, fill], axis=0).T.astype(bf16)
    aug[...] = a
    low = lax.broadcasted_iota(jnp.int32, (n, 128), 1) < HEAD_DIM
    qa[0] = jnp.where(low, q, a)
    qa[1] = jnp.where(low, a, q)
    doa[0] = jnp.where(low, do, a)
    doa[1] = jnp.where(low, a, do)
    q_t[...] = q.T
    do_t[...] = do.T


def prep_key(k, v, cj, ka_t, va_t, ca_t, k_t):
    n = k.shape[0]
    kt = k.T
    vt = v.T
    k_t[...] = kt
    row = lax.broadcasted_iota(jnp.int32, (128, n), 0)
    low = row < HEAD_DIM
    pos = jnp.where(low, row, row - HEAD_DIM)

    def pick(start):
        hit = (pos >= start) & (pos < start + 3)
        return jnp.where(hit, 1.0, 0.0).astype(bf16)

    ka_t[0] = jnp.where(low, kt, pick(0))
    ka_t[1] = jnp.where(low, pick(3), kt)
    va_t[0] = jnp.where(low, vt, pick(6))
    va_t[1] = jnp.where(low, pick(9), vt)
    c = [cj[d : d + 1, :] for d in range(3)]
    m = split3(c[0] * c[0] + c[1] * c[1] + c[2] * c[2])
    ca = jnp.concatenate(
        [jnp.zeros((12, n), f32)]
        + [-2.0 * x for x in c]
        + [jnp.ones((3, n), f32)]
        + list(m)
        + [jnp.zeros((128 - 21, n), f32)],
        axis=0,
    )
    ca_t[...] = ca.astype(bf16)


CHUNK = 256


def tile(parts, ka_t, va_t, ca_t, k_t, dk_t, dv_t, rates, ds):
    n = k_t.shape[1]
    pending = []

    def gradients(part, h, ii, jj, p, g):
        _, _, _, q_t, do_t, dq_t = part
        hh = pl.ds(h * HEAD_DIM, HEAD_DIM)
        dq_t[hh, ii] += dot(k_t[hh, jj], g, ((1,), (1,)))
        dv_t[hh, jj] += dot(do_t[hh, ii], p)
        dk_t[hh, jj] += dot(q_t[hh, ii], g)

    for part in parts:
        qa, doa, aug = part[:3]
        for i in range(0, n, CHUNK):
            for j in range(0, n, CHUNK):
                ii = pl.ds(i, CHUNK)
                jj = pl.ds(j, CHUNK)
                l2 = dot(aug[ii, :], ca_t[:, jj])
                lengths = l2 * lax.rsqrt(l2)
                for h in range(2):
                    s = dot(qa[h, ii, :], ka_t[h, :, jj])
                    gp = dot(doa[h, ii, :], va_t[h, :, jj])
                    p = jnp.exp2(s * (LOG2E / 8.0) - lengths * rates[h])
                    g = p * gp
                    ds[h] += jnp.sum((g * lengths).reshape(CHUNK // 8, 8, CHUNK), axis=0)
                    pending.append((part, h, ii, jj, p.astype(bf16), g.astype(bf16)))
                    if len(pending) > 1:
                        gradients(*pending.pop(0))
    gradients(*pending.pop(0))


START = [((q,), k) for q, k in ((0, 0), (0, 1), (0, 3), (1, 1), (3, 1), (2, 1))]
PAIRS = [((0, 1), 2), ((3, 2), 2), ((1, 3), 3)]
END = [((q,), k) for q, k in ((2, 3), (2, 0), (1, 0), (3, 0))]


def pick_at(t, values):
    out = jnp.int32(values[-1])
    for i in range(len(values) - 2, -1, -1):
        out = jnp.where(t <= i, jnp.int32(values[i]), out)
    return out


def place():
    seq = lax.axis_index("seq")
    head = lax.axis_index("head")
    return seq // 8, (seq // 2) % 4, seq % 2, head // 2, head % 2


def whole_kernel(
    query, key, value, attn_out, log_norm, d_output, out_weight, coords, slopes,
    d_query, d_key, d_value, d_weight, d_slopes,
    a_in, o_w, local_sem, piece, qs, dos, sm, kv, cj, sm_src, pair_src, w_part, w_send, w_x, w_sum, w_send_y, w_y, w_sum_y, w_z, w_all,
    aug, qa, doa, q_t, do_t, ka_t, va_t, ca_t, k_t, dq_t, dk_t, dv_t, ds,
    dq_send, dq_in, dkv_send, dkv_in, back_send, back_in, ds_send, ds_in,
    send_sem, recv_sem,
):
    rows = query.shape[0]
    n = 2 * rows
    y, z, xh, xl, c = place()
    head = xl * 2 + c

    def at(y, z, xh, xl, c):
        return ((y * 4 + z) * 2 + xh, xl * 2 + c)

    twin = at(y, z, xh, xl, 1 - c)
    near = at(y, z, xh, 1 - xl, c)
    far = at(y, z, 1 - xh, 1 - xl, c)
    across = at(y, z, 1 - xh, xl, c)

    def on_z(s):
        return at(y, (z + s) % 4, xh, xl, c)

    def on_y(s):
        return at((y + s) % 4, z, xh, xl, c)

    partners = [twin, near, far, across] + [on_z(s) for s in (1, 2, 3)] + [on_y(s) for s in (1, 2, 3)]
    barrier = pltpu.get_barrier_semaphore()
    for device in partners:
        pl.semaphore_signal(barrier, inc=1, device_id=device, device_id_type=pl.DeviceIdType.MESH)

    local = [
        pltpu.make_async_copy(src, dst, local_sem.at[i])
        for i, (src, dst) in enumerate(
            ((d_output, piece.at[head]), (out_weight, o_w), (attn_out, a_in))
        )
    ]
    for one in local:
        one.start()
    lane = lax.broadcasted_iota(jnp.int32, (1, rows), 1)
    pos = coords[...].astype(f32)
    for p in range(2):
        rate = jnp.where(lane < 128, slopes[2 * p], slopes[2 * p + 1])
        sm_src[p] = jnp.concatenate(
            [log_norm[2 * p : 2 * p + 2, :], jnp.zeros((2, rows), f32), pos, rate], axis=0
        )
    place_rows = jnp.concatenate([pos, jnp.zeros((5, rows), f32)], axis=0)
    cj[0, :, :rows] = place_rows
    cj[4, :, :rows] = place_rows
    pl.semaphore_wait(barrier, len(partners))

    count = [0]

    def link(src, dst, device):
        i = count[0]
        count[0] += 1
        return lambda: pltpu.make_async_remote_copy(
            src_ref=src,
            dst_ref=dst,
            send_sem=send_sem.at[i],
            recv_sem=recv_sem.at[i],
            device_id=device,
            device_id_type=pl.DeviceIdType.MESH,
        )

    def start(links):
        for one in links:
            one().start()

    def received(links):
        for one in links:
            one().wait_recv()

    first = pl.ds(0, rows)
    second = pl.ds(rows, rows)
    mine = pl.ds(pl.multiple_of(xh * 128, 128), 128)
    other = pl.ds(pl.multiple_of((1 - xh) * 128, 128), 128)

    own_out = [link(d_output, piece.at[head], near), link(d_output, piece.at[head], twin)]
    near_head = (1 - xl) * 2 + c
    forward = [link(piece.at[near_head], piece.at[near_head], twin)]
    near_kv = [
        link(array.at[:, mine], kv.at[0, i, first], near) for i, array in enumerate((key, value))
    ]
    far_kv = [
        link(array.at[:, other], kv.at[0, i, second], far) for i, array in enumerate((key, value))
    ]
    far_kv += [link(cj.at[4, :, first], cj.at[0, :, second], far)]
    near_q = [link(query.at[:, mine], qs.at[0, first], near)]
    far_q = [link(query.at[:, other], qs.at[0, second], far)]
    cross_do = [
        link(pair_src.at[xh], dos.at[0, first], near),
        link(pair_src.at[1 - xh], dos.at[0, second], far),
        link(sm_src.at[xh], sm.at[0, :, first], near),
        link(sm_src.at[1 - xh], sm.at[0, :, second], far),
    ]
    gather_kv = {
        s: [link(kv.at[0], kv.at[s], on_y(s)), link(cj.at[0], cj.at[s], on_y(s))] for s in (1, 3)
    }
    gather_q = {s: [link(qs.at[0], qs.at[s], on_z(s))] for s in (1, 3)}
    gather_do = {
        s: [link(dos.at[0], dos.at[s], on_z(s)), link(sm.at[0], sm.at[s], on_z(s))] for s in (1, 3)
    }
    relay_kv = {
        s: [
            link(kv.at[s, :, half], kv.at[2, :, half], on_y(s)),
            link(cj.at[s, :, half], cj.at[2, :, half], on_y(s)),
        ]
        for s, half in ((1, first), (3, second))
    }
    relay_q = {
        s: [
            link(qs.at[s, half], qs.at[2, half], on_z(s)),
            link(dos.at[s, half], dos.at[2, half], on_z(s)),
            link(sm.at[s, :, half], sm.at[2, :, half], on_z(s)),
        ]
        for s, half in ((1, first), (3, second))
    }
    give_q = {s: [link(dq_send.at[s], dq_in.at[s], on_z(4 - s))] for s in (1, 3, 2)}
    give_kv = {s: [link(dkv_send.at[s], dkv_in.at[s], on_y(4 - s))] for s in (1, 3, 2)}
    w_rs_x = [link(w_send, w_x, across)]
    w_rs_y = [link(w_send_y.at[(y + s) % 4], w_y.at[s], on_y(s)) for s in (1, 3, 2)]
    w_rs_z = [link(w_sum_y.at[(z + s) % 4], w_z.at[s], on_z(s)) for s in (1, 3, 2)]
    w_ag_z = [link(w_all.at[xh, y, z], w_all.at[xh, y, z], on_z(s)) for s in (1, 3, 2)]
    w_ag_y = [link(w_all.at[xh, y], w_all.at[xh, y], on_y(s)) for s in (1, 3, 2)]
    w_ag_x = [link(w_all.at[xh], w_all.at[xh], across)]
    back = [
        [
            link(back_send.at[i, :, first], back_in.at[i, xh], near),
            link(back_send.at[i, :, second], back_in.at[i, xh], far),
        ]
        for i in range(3)
    ]
    ds_z = [link(ds_send.at[0], ds_in.at[0, s], on_z(s)) for s in (1, 3, 2)]
    ds_y = [link(ds_send.at[1], ds_in.at[1, s], on_y(s)) for s in (1, 3, 2)]
    ds_x = [
        link(ds_send.at[2], ds_in.at[2, xh], near),
        link(ds_send.at[2], ds_in.at[2, xh], far),
    ]

    start(far_kv)
    start(near_kv)
    start(far_q)
    start(own_out[1:])
    for one in near_kv:
        one().wait_send()
    start(own_out[:1])
    dq_t[...] = jnp.zeros_like(dq_t)
    dk_t[...] = jnp.zeros_like(dk_t)
    dv_t[...] = jnp.zeros_like(dv_t)
    ds[...] = jnp.zeros_like(ds)
    received(far_kv)
    received(near_kv)
    for s in (1, 3):
        start(gather_kv[s])
    def prepare_key(s):
        prep_key(kv[s, 0], kv[s, 1], cj[s], ka_t.at[s], va_t.at[s], ca_t.at[s], k_t.at[s])

    prepare_key(0)
    received(own_out[:1])
    start(forward)
    start(near_q)
    received(own_out[1:])
    received(forward)
    for one in local:
        one.wait()
    total = jnp.zeros((rows, 256), f32)
    for g in range(4):
        total = total + dot(piece[g], o_w[:, g * 256 : (g + 1) * 256], ((1,), (1,)))
    d_attn = total.astype(bf16)
    product = (d_attn.astype(f32) * a_in[...].astype(f32)).T
    for p in range(2):
        pair_src[p] = d_attn[:, p * 128 : (p + 1) * 128]
        for h in range(2):
            r = (2 * p + h) * HEAD_DIM
            sm_src[p, 2 + h : 3 + h, :] = jnp.sum(product[r : r + HEAD_DIM], axis=0, keepdims=True)
    start(cross_do)
    received(far_q)
    received(near_q)
    for s in (1, 3):
        start(gather_q[s])
    a_t = a_in[...].T
    for g in range(4):
        part = dot(a_t, piece[g])
        w_part[g // 2, :, :, :, (g % 2) * 256 : (g % 2 + 1) * 256] = part.reshape(4, 4, 16, 256)
    w_send[...] = w_part[1 - xh].astype(bf16)
    received(cross_do)
    for s in (1, 3):
        start(gather_do[s])
    start(w_rs_x)

    def prepare_query(s):
        prep_query(
            qs[s], dos[s], sm[s], aug.at[s], qa.at[s], doa.at[s], q_t.at[s], do_t.at[s]
        )

    prepare_query(0)
    rates = [
        jnp.concatenate([sm[0, 7:8, h * 128 : (h + 1) * 128]] * (CHUNK // 128), axis=1) * LOG2E
        for h in range(2)
    ]

    def take_key(s):
        received(gather_kv[s])
        start(relay_kv[s])
        prepare_key(s)

    def take_queries():
        for s in (1, 3):
            received(gather_q[s])
            received(gather_do[s])
            start(relay_q[s])
        prepare_query(1)

    def far_key():
        received(relay_kv[1])
        received(relay_kv[3])
        prepare_key(2)

    def far_query():
        received(relay_q[1])
        received(relay_q[3])
        prepare_query(2)

    def send_kv(s):
        dkv_send[s, 0] = dk_t[s].astype(bf16)
        dkv_send[s, 1] = dv_t[s].astype(bf16)
        start(give_kv[s])

    def send_q(s):
        dq_send[s] = dq_t[s].astype(bf16)
        start(give_q[s])

    def weight_x():
        received(w_rs_x)
        w_sum[...] = w_part[xh] + w_x[...].astype(f32)
        w_send_y[...] = w_sum[...].astype(bf16)
        start(w_rs_y)

    def weight_y():
        received(w_rs_y)
        total = w_sum[y]
        for s in (1, 2, 3):
            total = total + w_y[s].astype(f32)
        w_sum_y[...] = total
        start(w_rs_z)

    def weight_z():
        received(w_rs_z)
        w_all[xh, y, z] = (w_sum_y[z] + w_z[1] + w_z[2] + w_z[3]).astype(bf16)
        start(w_ag_z)

    def weight_gather_y():
        received(w_ag_z)
        start(w_ag_y)

    def weight_gather_x():
        received(w_ag_y)
        start(w_ag_x)

    def add_kv(s):
        received(give_kv[s])
        dk_t[0] += dkv_in[s, 0].astype(f32)
        dv_t[0] += dkv_in[s, 1].astype(f32)

    def add_q(s):
        received(give_q[s])
        dq_t[0] += dq_in[s].astype(f32)

    before = {
        1: [lambda: take_key(1)],
        2: [lambda: take_key(3)],
        3: [take_queries],
        4: [weight_x, lambda: prepare_query(3)],
        5: [far_query],
        6: [weight_y, lambda: send_kv(1), far_key],
        8: [weight_z],
        10: [weight_gather_y, lambda: send_kv(2)],
        12: [weight_gather_x],
        13: [lambda: send_kv(3)],
        14: [lambda: send_q(2)],
        15: [lambda: send_q(1), lambda: add_kv(1), lambda: add_kv(2)],
    }

    def run_events(t, steps):
        if len(steps) == 1:
            for event in before.get(steps[0], []):
                event()
        else:
            middle = len(steps) // 2
            lax.cond(
                t < steps[middle],
                lambda: run_events(t, steps[:middle]),
                lambda: run_events(t, steps[middle:]),
            )

    def blocks(order, first_step):
        width = len(order[0][0])
        steps = [first_step + i * width for i in range(len(order))]

        def block(i, _):
            run_events(first_step + i * width, steps)
            sj = pick_at(i, [k for _, k in order])
            parts = []
            for m in range(width):
                si = pick_at(i, [q[m] for q, _ in order])
                parts.append([x.at[si] for x in (qa, doa, aug, q_t, do_t, dq_t)])
            tile(
                parts, ka_t.at[sj], va_t.at[sj], ca_t.at[sj], k_t.at[sj], dk_t.at[sj], dv_t.at[sj],
                rates, ds,
            )
            return 0

        lax.fori_loop(0, len(order), block, 0)
        return first_step + len(order) * width

    step = blocks(START, 0)
    step = blocks(PAIRS, step)
    blocks(END, step)
    send_q(3)

    rates_sum = [
        jnp.sum(jnp.sum(-ds[h], axis=0, keepdims=True), axis=1, keepdims=True) for h in range(2)
    ]
    ds_send[0] = jnp.concatenate(
        [jnp.broadcast_to(r, (1, 128)) for r in rates_sum] + [jnp.zeros((6, 128), f32)], axis=0
    )
    start(ds_z)
    add_kv(3)
    back_send[2] = dv_t[0].astype(bf16)
    start(back[2])
    back_send[1] = (dk_t[0] * 0.125).astype(bf16)
    start(back[1])
    received(ds_z)
    ds_send[1] = ds_send[0] + ds_in[0, 1] + ds_in[0, 2] + ds_in[0, 3]
    start(ds_y)
    add_q(2)
    add_q(1)
    received(ds_y)
    ds_send[2] = ds_send[1] + ds_in[1, 1] + ds_in[1, 2] + ds_in[1, 3]
    start(ds_x)
    add_q(3)
    back_send[0] = (dq_t[0] * 0.125).astype(bf16)
    start(back[0])
    for i, out in ((2, d_value), (1, d_key), (0, d_query)):
        received(back[i])
        for p in range(2):
            out[:, p * 128 : (p + 1) * 128] = back_in[i, p].T
    received(w_ag_x)
    for i in range(2):
        d_weight[:, i * 512 : (i + 1) * 512] = w_all[i].reshape(256, 512)
    received(ds_x)
    d_slopes[...] = jnp.concatenate([ds_in[2, 0, 0:2], ds_in[2, 1, 0:2]], axis=0)

    sent = [own_out, forward, far_kv, far_q, near_q, cross_do]
    sent += [w_rs_x, w_rs_z, w_rs_y, w_ag_y, w_ag_z, w_ag_x]
    sent += [group[s] for group in (give_q, give_kv) for s in (1, 2, 3)]
    groups = (gather_kv, gather_q, gather_do, relay_kv, relay_q)
    sent += [group[s] for group in groups for s in (1, 3)]
    sent += back + [ds_z, ds_y, ds_x]
    for links in sent:
        for one in links:
            one().wait_send()


LINKS = 68


def hand_over(q, k, v, w, s, d_query, d_key, d_value, d_weight, d_slopes):
    d_query[...] = q[...]
    d_key[...] = k[...]
    d_value[...] = v[...]
    d_weight[...] = w[...].astype(f32)
    for i in range(4):
        d_slopes[i] = s[i, 0]


def per_device(query, key, value, attn_out, log_norm, d_output, out_weight, coords, slopes):
    rows, cols = query.shape
    n = 2 * rows
    vm = pl.BlockSpec(memory_space=pltpu.VMEM)
    part = (4, 4, out_weight.shape[0] // 16, out_weight.shape[1] // 2)

    def wide(*lead):
        return pltpu.VMEM(lead + (n, 128), bf16)

    def tall(dtype, *lead):
        return pltpu.VMEM(lead + (128, n), dtype)

    scratch = [
        pltpu.VMEM((rows, cols), bf16), pltpu.VMEM(out_weight.shape, bf16),
        pltpu.SemaphoreType.DMA((3,)),
        pltpu.VMEM((4, rows, cols), bf16),
        wide(4), wide(4),
        pltpu.VMEM((4, 8, n), f32),
        wide(4, 2),
        pltpu.VMEM((5, 8, n), f32),
        pltpu.VMEM((2, 8, rows), f32),
        pltpu.VMEM((2, rows, 128), bf16),
        pltpu.VMEM((2,) + part, f32),
        pltpu.VMEM(part, bf16), pltpu.VMEM(part, bf16),
        pltpu.VMEM(part, f32),
        pltpu.VMEM(part, bf16), pltpu.VMEM(part, bf16),
        pltpu.VMEM(part[1:], f32), pltpu.VMEM(part[1:], f32),
        pltpu.VMEM((2,) + part, bf16),
        wide(4), wide(4, 2), wide(4, 2), tall(bf16, 4), tall(bf16, 4),
        tall(bf16, 4, 2), tall(bf16, 4, 2), tall(bf16, 4), tall(bf16, 4),
        tall(f32, 4), tall(f32, 4), tall(f32, 4), pltpu.VMEM((2, 8, CHUNK), f32),
        tall(bf16, 4), tall(bf16, 4),
        tall(bf16, 4, 2), tall(bf16, 4, 2),
        tall(bf16, 3), pltpu.VMEM((3, 2, 128, rows), bf16),
        pltpu.VMEM((3, 8, 128), f32), pltpu.VMEM((3, 4, 8, 128), f32),
        pltpu.SemaphoreType.DMA((LINKS,)), pltpu.SemaphoreType.DMA((LINKS,)),
    ]
    hbm = pl.BlockSpec(memory_space=pl.ANY)
    smem = pl.BlockSpec(memory_space=pltpu.SMEM)
    results = pl.pallas_call(
        whole_kernel,
        out_shape=[jax.ShapeDtypeStruct((rows, cols), bf16)] * 3
        + [jax.ShapeDtypeStruct(out_weight.shape, bf16), jax.ShapeDtypeStruct((4, 128), f32)],
        in_specs=[hbm] * 4 + [vm] + [hbm] * 2 + [vm, smem],
        out_specs=[vm] * 5,
        scratch_shapes=scratch,
        compiler_params=pltpu.CompilerParams(
            collective_id=0, has_side_effects=True, vmem_limit_bytes=60 << 20
        ),
        name="whole",
    )(query, key, value, attn_out, log_norm, d_output, out_weight, coords, slopes)
    return pl.pallas_call(
        hand_over,
        out_shape=[jax.ShapeDtypeStruct((rows, cols), bf16)] * 3
        + [jax.ShapeDtypeStruct(out_weight.shape, f32), jax.ShapeDtypeStruct(slopes.shape, f32)],
        in_specs=[vm] * 4 + [smem],
        out_specs=[vm] * 4 + [smem],
        compiler_params=pltpu.CompilerParams(vmem_limit_bytes=60 << 20),
        name="hand_over",
    )(*results)


def solution(mesh):
    placed = (
        P("seq", "head"),
        P("seq", "head"),
        P("seq", "head"),
        P("seq", "head"),
        P("head", "seq"),
        P("seq", "head"),
        P("head", None),
        P(None, "seq"),
        P("head"),
    )
    return jax.shard_map(
        per_device,
        mesh=mesh,
        in_specs=placed,
        out_specs=(
            P("seq", "head"),
            P("seq", "head"),
            P("seq", "head"),
            P("head", None),
            P("head"),
        ),
        check_vma=False,
    )
```
